512 devices in a mesh: loop: 64 (over z_lo, x, core), grp: 8 (over y, z_hi).
Axes of the slice: x: 4, y: 4, z: 16 (z_hi: 2, z_lo: 8; z = z_hi * 8 + z_lo), core: 2. Of those that a mesh axis runs over, the one named last changes fastest.
Arguments:
- picture_vectors: float32 [12288, 1152], P(('loop', 'grp')), may hold values from -0.8249579 to 0.8249579, as said below
- caption_vectors: float32 [12288, 1152], P(('loop', 'grp')), may hold values from -0.8249579 to 0.8249579, as said below
- heat_exponent: float32 [1], replicated, may hold values from 2 to 2.6
- offset_added: float32 [1], replicated, may hold values from -9 to -7
Outputs:
- loss_mean: float32 [1], replicated
- image_grads: float32 [12288, 1152], P(('loop', 'grp'))
- text_grads: float32 [12288, 1152], P(('loop', 'grp'))
The draws below stay inside these ranges and needn't reach their ends.
Inputs may be any that keep to these rules, and one draw needn't show every extreme that they name: `picture_vectors`: entries of image embeddings lie within the stated bounds. `caption_vectors`: entries of text embeddings lie within the stated bounds.
All inputs are finite; a program needn't handle non-finite values.
Results may differ from the reference program's by a relative error of at most 0.0031.
Values may be sent and summed in bfloat16 or wider, within the bound.
No kernel may reach another device: no remote copies, remote signals or barrier semaphores. Data moves between devices by JAX's collectives and lax.ppermute only.
A program may use at most 64 MiB of HBM per device.

```python
import math
import jax
import jax.numpy as jnp
from jax import lax

DIM = 1152
CLUSTERS = 16
TOTAL = 12288


def shared_parts(key):
    centers = jax.random.truncated_normal(jax.random.fold_in(key, 101), -4.0, 4.0, (CLUSTERS, DIM), jnp.float32)
    member = jax.random.randint(jax.random.fold_in(key, 102), (TOTAL,), 0, CLUSTERS)
    pair_base = jax.random.truncated_normal(jax.random.fold_in(key, 103), -4.0, 4.0, (TOTAL, DIM), jnp.float32)
    return 0.6 * (centers[member] + pair_base)


def noisy_rows(key, common):
    own_noise = jax.random.truncated_normal(jax.random.fold_in(key, 7), -4.0, 4.0, (TOTAL, DIM), jnp.float32)
    return (common + 0.5 * own_noise) * DIM ** (-0.5)


def draw_picture_vectors(key, part):
    common = shared_parts(key)
    key = jax.random.fold_in(key, 1)
    return noisy_rows(key, common)


def draw_caption_vectors(key, part):
    common = shared_parts(key)
    key = jax.random.fold_in(key, 2)
    return noisy_rows(key, common)


def setup_inputs(seed: int = 0) -> dict:
    streams_of = jax.random.split(jax.random.key(seed), 5)
    return {
        "picture_vectors": draw_picture_vectors(jax.random.fold_in(streams_of[4], 71), 0),
        "caption_vectors": draw_caption_vectors(jax.random.fold_in(streams_of[4], 71), 0),
        "heat_exponent": jnp.clip(jax.random.uniform(streams_of[2], (1,), jnp.float32, 2.0, 2.6), 2.0, 2.6),
        "offset_added": jnp.clip(jax.random.uniform(streams_of[3], (1,), jnp.float32, -9.0, -7.0), -9.0, -7.0),
    }


epsilon = 1e-06

def normalize(raw_rows):
    row_norm = jnp.sqrt(lax.optimization_barrier(jnp.sum(raw_rows * raw_rows, axis=1, keepdims=True)) + epsilon)
    return (raw_rows / row_norm, row_norm)

def back_norm(unit_rows, row_norm, gradient):
    return (gradient - unit_rows * lax.optimization_barrier(jnp.sum(unit_rows * gradient, axis=1, keepdims=True))) / row_norm

def reference(picture_vectors, caption_vectors, heat_exponent, offset_added):
    heat_multiplier = jnp.exp(heat_exponent[0])
    cyclic_shift_count = offset_added[0]
    image_unit, image_norm = normalize(picture_vectors)
    text_unit, text_norm = normalize(caption_vectors)
    image_low = image_unit.astype(jnp.bfloat16)
    caption_start_index = text_unit.astype(jnp.bfloat16)
    block_rows = math.gcd(TOTAL, 512)
    block_count = TOTAL // block_rows
    text_identifiers = jnp.arange(TOTAL, dtype=jnp.int32)

    def one_block(state_tuple, block_index):
        text_sum, loss_sum = state_tuple
        first_row = (block_index * block_rows).astype(jnp.int32)
        picture_share = lax.dynamic_slice_in_dim(image_low, first_row, block_rows, 0)
        match_logits = jnp.dot(picture_share, caption_start_index.T, preferred_element_type=jnp.float32) * heat_multiplier + cyclic_shift_count
        image_identifiers = first_row + jnp.arange(block_rows, dtype=jnp.int32)
        match_targets = jnp.where(image_identifiers[:, None] == text_identifiers[None, :], 1.0, -1.0).astype(match_logits.dtype)
        loss_sum = loss_sum + jnp.sum(jax.nn.softplus(-match_targets * match_logits))
        match_factors = (-match_targets * jax.nn.sigmoid(-match_targets * match_logits) * heat_multiplier).astype(jnp.bfloat16)
        image_grad = jnp.dot(match_factors, caption_start_index, preferred_element_type=jnp.float32)
        text_sum = text_sum + jnp.dot(match_factors.T, picture_share, preferred_element_type=jnp.float32)
        return ((text_sum, loss_sum), image_grad)
    start_state = (jnp.zeros(caption_vectors.shape, jnp.float32), jnp.zeros((), jnp.float32))
    (text_sum, loss_sum), image_blocks = lax.scan(one_block, start_state, jnp.arange(block_count, dtype=jnp.int32))
    image_sum = image_blocks.reshape(TOTAL, DIM)
    loss_mean = (loss_sum / TOTAL).reshape(1)
    return (loss_mean, back_norm(image_unit, image_norm, image_sum), back_norm(text_unit, text_norm, text_sum))
```

```python
import functools

import jax
import jax.numpy as jnp
from jax import lax
from jax.experimental import pallas as pl
from jax.experimental.pallas import tpu as pltpu
from jax.sharding import Mesh, PartitionSpec as P

epsilon = 1e-06
AXES = ("zl", "x", "c", "y", "zh")
SIZES = (8, 4, 2, 4, 2)
RING = ("zl", "zh")
PLANE = ("x", "y")
LANES = 128
LIMIT = 48 * 1024 * 1024


def normalize(raw_rows):
    row_norm = jnp.sqrt(jnp.sum(raw_rows * raw_rows, axis=1, keepdims=True) + epsilon)
    return (raw_rows / row_norm, row_norm)


def back_norm(unit_rows, row_norm, gradient):
    return (gradient - unit_rows * jnp.sum(unit_rows * gradient, axis=1, keepdims=True)) / row_norm


def low(rows):
    return rows.astype(jnp.bfloat16).astype(jnp.float32)


def loss_and_sigmoid(values):
    small = jnp.exp(-jnp.abs(values))
    loss = jnp.maximum(values, 0.0) + jnp.log1p(small)
    return loss, jnp.where(values >= 0, 1.0, small) / (1.0 + small)


def own_pairs(image_low, text_low, heat, offset):
    return jnp.sum(image_low * text_low, axis=1, keepdims=True) * heat + offset


def unit_kernel(heat_ref, offset_ref, picture_ref, caption_ref, image_ref, text_ref, loss_ref):
    image_unit, _ = normalize(picture_ref[...])
    text_unit, _ = normalize(caption_ref[...])
    image_low, text_low = image_unit.astype(jnp.bfloat16), text_unit.astype(jnp.bfloat16)
    image_ref[...] = image_low
    text_ref[...] = text_low
    heat = jnp.exp(jnp.full((1, 1), heat_ref[0], jnp.float32))
    logits = own_pairs(image_low.astype(jnp.float32), text_low.astype(jnp.float32), heat, offset_ref[0])
    loss, _ = loss_and_sigmoid(-logits)
    loss_ref[...] = loss


def unit_rows(heat_exponent, offset_added, pictures, captions):
    rows = pictures.shape[0]
    return pl.pallas_call(
        unit_kernel,
        in_specs=[pl.BlockSpec(memory_space=pltpu.SMEM)] * 2 + [pl.BlockSpec(memory_space=pltpu.VMEM)] * 2,
        out_shape=[
            jax.ShapeDtypeStruct(pictures.shape, jnp.bfloat16),
            jax.ShapeDtypeStruct(captions.shape, jnp.bfloat16),
            jax.ShapeDtypeStruct((rows, 1), jnp.float32),
        ],
    )(heat_exponent, offset_added, pictures, captions)


def pair_kernel(
    rows, places, heat_ref, offset_ref, own_loss_ref, image_ref, text_ref,
    image_out_ref, text_out_ref, text_sum_ref, loss_sum_ref,
):
    step = pl.program_id(0)
    images = image_ref[...]
    texts = text_ref[...]
    heat = jnp.exp(jnp.full((1, 1), heat_ref[0], jnp.float32))
    logits = lax.dot_general(
        images, texts, (((1,), (1,)), ((), ())), preferred_element_type=jnp.float32
    )
    logits = logits * heat + offset_ref[0]
    image_row = lax.broadcasted_iota(jnp.int32, logits.shape, 0) - places[1] * rows
    text_row = lax.broadcasted_iota(jnp.int32, logits.shape, 1) - places[2] * rows
    match = (image_row == text_row) & (image_row >= 0) & (image_row < rows) & (step == 1)
    loss, sigmoid = loss_and_sigmoid(logits)
    weights = jnp.where(match, 0.0, heat * sigmoid).astype(jnp.bfloat16)
    loss = jnp.sum(jnp.where(match, 0.0, loss), axis=0, keepdims=True)
    image_out_ref[...] = jnp.dot(weights, texts, preferred_element_type=jnp.float32)[None]
    text_part = lax.dot_general(
        weights, images, (((0,), (0,)), ((), ())), preferred_element_type=jnp.float32
    )

    @pl.when(step == 0)
    def _():
        text_sum_ref[...] = text_part
        loss_sum_ref[...] = loss

    @pl.when(step == 1)
    def _():
        width = text_part.shape[1]
        text_out_ref[:, :width] = (text_sum_ref[...] + text_part).astype(jnp.bfloat16)
        total = jnp.sum(loss_sum_ref[...] + loss, axis=1, keepdims=True)
        total += jnp.sum(own_loss_ref[...], axis=0, keepdims=True)
        text_out_ref[:, width:] = pieces(total, (text_out_ref.shape[0], LANES))


def pieces(total, shape):
    first = low(total)
    second = low(total - first)
    third = total - first - second
    lane = lax.broadcasted_iota(jnp.int32, shape, len(shape) - 1)
    spread = jnp.where(lane == 0, first, jnp.where(lane == 1, second, jnp.where(lane == 2, third, 0.0)))
    return spread.astype(jnp.bfloat16)


def pair_terms(rows, places, heat_exponent, offset_added, own_loss, images, texts):
    half, width = images.shape[0] // 2, images.shape[1]
    count = texts.shape[0]
    return pl.pallas_call(
        functools.partial(pair_kernel, rows),
        grid_spec=pltpu.PrefetchScalarGridSpec(
            num_scalar_prefetch=1,
            grid=(2,),
            in_specs=[
                pl.BlockSpec(memory_space=pltpu.SMEM),
                pl.BlockSpec(memory_space=pltpu.SMEM),
                pl.BlockSpec((rows, 1), lambda i, p: (0, 0)),
                pl.BlockSpec((half, width), lambda i, p: (jnp.where(i == 0, 1 - p[0], p[0]), 0)),
                pl.BlockSpec((count, width), lambda i, p: (0, 0)),
            ],
            out_specs=[
                pl.BlockSpec((1, half, width), lambda i, p: (i, 0, 0)),
                pl.BlockSpec((count, width + LANES), lambda i, p: (0, 0)),
            ],
            scratch_shapes=[
                pltpu.VMEM((count, width), jnp.float32),
                pltpu.VMEM((1, count), jnp.float32),
            ],
        ),
        out_shape=[
            jax.ShapeDtypeStruct((2, half, width), jnp.float32),
            jax.ShapeDtypeStruct((count, width + LANES), jnp.bfloat16),
        ],
        compiler_params=pltpu.CompilerParams(vmem_limit_bytes=LIMIT),
        cost_estimate=pl.CostEstimate(
            flops=12 * half * count * width, bytes_accessed=16 * half * width, transcendentals=6 * half * count
        ),
    )(places, heat_exponent, offset_added, own_loss, images, texts)


def grad_kernel(heat_ref, offset_ref, picture_ref, caption_ref, image_part_ref, text_part_ref, image_ref, text_ref):
    width = picture_ref.shape[1]
    image_unit, image_norm = normalize(picture_ref[...])
    text_unit, text_norm = normalize(caption_ref[...])
    image_low, text_low = low(image_unit), low(text_unit)
    heat = jnp.exp(jnp.full((1, 1), heat_ref[0], jnp.float32))
    _, sigmoid = loss_and_sigmoid(-own_pairs(image_low, text_low, heat, offset_ref[0]))
    weights = low(-sigmoid * heat)
    image_sum = weights * text_low
    text_sum = weights * image_low
    for part in range(image_part_ref.shape[0]):
        image_sum += image_part_ref[part, :, :width].astype(jnp.float32)
    for part in range(text_part_ref.shape[0]):
        text_sum += text_part_ref[part, :, :width].astype(jnp.float32)
    image_ref[...] = back_norm(image_unit, image_norm, image_sum)
    text_ref[...] = back_norm(text_unit, text_norm, text_sum)


def gradients(heat_exponent, offset_added, pictures, captions, image_parts, text_parts):
    return pl.pallas_call(
        grad_kernel,
        in_specs=[pl.BlockSpec(memory_space=pltpu.SMEM)] * 2 + [pl.BlockSpec(memory_space=pltpu.VMEM)] * 4,
        out_shape=[jax.ShapeDtypeStruct(pictures.shape, jnp.float32)] * 2,
        compiler_params=pltpu.CompilerParams(vmem_limit_bytes=LIMIT),
    )(heat_exponent, offset_added, pictures, captions, image_parts, text_parts)


def gathered(block, axes):
    count = lax.axis_size(axes)
    return lax.all_to_all(jnp.broadcast_to(block[None], (count, *block.shape)), axes, 0, 0)


def loss_in(parts, width):
    return jnp.sum(parts[:, 0, width : width + 3].astype(jnp.float32))


def shards(picture_vectors, caption_vectors, heat_exponent, offset_added):
    rows, width = picture_vectors.shape
    ring = lax.axis_size(RING)
    plane = lax.axis_size(PLANE)
    image_low, text_low, own_loss = unit_rows(heat_exponent, offset_added, picture_vectors, caption_vectors)
    images = gathered(image_low, RING).reshape(ring * rows, width)
    images = lax.all_gather(images, "c", axis=0, tiled=True)
    texts = gathered(text_low, PLANE).reshape(plane * rows, width)
    core = lax.axis_index("c")
    places = jnp.stack([core, lax.axis_index(RING), lax.axis_index(PLANE)]).astype(jnp.int32)
    image_halves, text_part = pair_terms(rows, places, heat_exponent, offset_added, own_loss, images, texts)
    image_other = lax.ppermute(image_halves[0], "c", [(0, 1), (1, 0)])
    text_parts = lax.all_to_all(text_part.reshape(plane, rows, width + LANES), PLANE, 0, 0)
    image_part = (image_halves[1] + image_other).astype(jnp.bfloat16).reshape(ring, rows, width)
    loss_block = pieces(loss_in(text_parts, width), (ring, rows, LANES))
    image_parts = lax.all_to_all(jnp.concatenate([image_part, loss_block], axis=2), RING, 0, 0)
    loss_total = lax.psum(loss_in(image_parts, width), "c")
    loss_mean = (loss_total / (rows * lax.axis_size(AXES))).reshape(1)
    image_grads, text_grads = gradients(
        heat_exponent, offset_added, picture_vectors, caption_vectors, image_parts, text_parts
    )
    return (loss_mean, image_grads, text_grads)


def solution(mesh):
    fine = Mesh(mesh.devices.reshape(SIZES), AXES)
    in_specs = (P(AXES, None), P(AXES, None), P(), P())
    out_specs = (P(), P(AXES, None), P(AXES, None))
    return jax.shard_map(shards, mesh=fine, in_specs=in_specs, out_specs=out_specs, check_vma=False)
```

```python
import jax
import jax.numpy as jnp
from jax import lax
from jax.experimental import pallas as pl
from jax.experimental.pallas import tpu as pltpu
from jax.sharding import Mesh, PartitionSpec as P

epsilon = 1e-06
AXES = ("zl", "x", "c", "y", "zh")
SIZES = (8, 4, 2, 4, 2)
PLANE = ("x", "y")
COLUMN = ("zl", "c", "zh")
LANES = 128
CHUNK = 256
LIMIT = 48 * 1024 * 1024
HALF = 0.5


def normalize(raw_rows):
    row_norm = jnp.sqrt(jnp.sum(raw_rows * raw_rows, axis=1, keepdims=True) + epsilon)
    return (raw_rows / row_norm, row_norm)


def back_norm(unit_rows, row_norm, gradient):
    return (gradient - unit_rows * jnp.sum(unit_rows * gradient, axis=1, keepdims=True)) / row_norm


def low(rows):
    return rows.astype(jnp.bfloat16).astype(jnp.float32)


def loss_and_sigmoid(values):
    small = jnp.exp(-jnp.abs(values))
    loss = jnp.maximum(values, 0.0) + jnp.log1p(small)
    return loss, jnp.where(values >= 0, 1.0, small) / (1.0 + small)


def own_pairs(image_low, text_low, heat, offset):
    return jnp.sum(image_low * text_low, axis=1, keepdims=True) * heat + offset


def unit_kernel(heat_ref, offset_ref, picture_ref, caption_ref, image_ref, text_ref, loss_ref):
    image_unit, _ = normalize(picture_ref[...])
    text_unit, _ = normalize(caption_ref[...])
    image_low, text_low = image_unit.astype(jnp.bfloat16), text_unit.astype(jnp.bfloat16)
    image_ref[...] = image_low
    text_ref[...] = text_low
    heat = jnp.exp(jnp.full((1, 1), heat_ref[0], jnp.float32))
    logits = own_pairs(image_low.astype(jnp.float32), text_low.astype(jnp.float32), heat, offset_ref[0])
    loss, _ = loss_and_sigmoid(-logits)
    loss_ref[...] = loss


def unit_rows(heat_exponent, offset_added, pictures, captions):
    rows = pictures.shape[0]
    return pl.pallas_call(
        unit_kernel,
        in_specs=[pl.BlockSpec(memory_space=pltpu.SMEM)] * 2 + [pl.BlockSpec(memory_space=pltpu.VMEM)] * 2,
        out_shape=[
            jax.ShapeDtypeStruct(pictures.shape, jnp.bfloat16),
            jax.ShapeDtypeStruct(captions.shape, jnp.bfloat16),
            jax.ShapeDtypeStruct((rows, 1), jnp.float32),
        ],
    )(heat_exponent, offset_added, pictures, captions)


def pieces(total, shape):
    first = low(total)
    second = low(total - first)
    third = total - first - second
    lane = lax.broadcasted_iota(jnp.int32, shape, len(shape) - 1)
    spread = jnp.where(lane == 0, first, jnp.where(lane == 1, second, jnp.where(lane == 2, third, 0.0)))
    return spread.astype(jnp.bfloat16)


def pair_kernel(
    place_ref, heat_ref, offset_ref, own_loss_ref, near_ref, far_ref, text_ref,
    near_out_ref, far_out_ref, text_out_ref, loss_sum_ref,
):
    step = pl.program_id(0)
    rows = own_loss_ref.shape[0]
    half, width = near_ref.shape
    texts = text_ref[...]
    count = texts.shape[0]
    heat = jnp.exp(jnp.full((1, 1), heat_ref[0], jnp.float32))
    image_parts = []
    text_part = jnp.zeros((count, width), jnp.float32)
    loss = jnp.zeros((1, count), jnp.float32)
    for images in (near_ref[...], far_ref[...]):
        logits = lax.dot_general(
            images, texts, (((1,), (1,)), ((), ())), preferred_element_type=jnp.float32
        )
        logits = logits * heat + offset_ref[0]
        loss_part, sigmoid = loss_and_sigmoid(logits)
        weights = heat * sigmoid
        if not image_parts:
            image_row = lax.broadcasted_iota(jnp.int32, logits.shape, 0)
            text_row = lax.broadcasted_iota(jnp.int32, logits.shape, 1) + (step * count - place_ref[0])
            match = (image_row == text_row) & (image_row < rows)
            weights = jnp.where(match, 0.0, weights)
            loss_part = jnp.where(match, 0.0, loss_part)
        weights = weights.astype(jnp.bfloat16)
        loss += jnp.sum(loss_part, axis=0, keepdims=True)
        image_parts.append(jnp.dot(weights, texts, preferred_element_type=jnp.float32))
        text_part += lax.dot_general(
            weights, images, (((0,), (0,)), ((), ())), preferred_element_type=jnp.float32
        )
    start = pl.multiple_of(step * count, count)
    text_out_ref[pl.ds(start, count), :width] = text_part.astype(jnp.bfloat16)

    @pl.when(step == 0)
    def _():
        near_out_ref[...] = image_parts[0]
        far_out_ref[...] = image_parts[1]
        loss_sum_ref[...] = loss

    @pl.when(step > 0)
    def _():
        near_out_ref[...] += image_parts[0]
        far_out_ref[...] += image_parts[1]
        loss_sum_ref[...] += loss

    @pl.when(step == pl.num_programs(0) - 1)
    def _():
        total = jnp.sum(loss_sum_ref[...], axis=1, keepdims=True)
        total += jnp.sum(own_loss_ref[...], axis=0, keepdims=True)
        text_out_ref[:, width:] = pieces(total, (text_out_ref.shape[0], LANES))


def pair_terms(place, heat_exponent, offset_added, own_loss, near, far, texts):
    half, width = near.shape
    count = texts.shape[0]
    return pl.pallas_call(
        pair_kernel,
        grid=(count // CHUNK,),
        in_specs=[pl.BlockSpec(memory_space=pltpu.SMEM)] * 3
        + [
            pl.BlockSpec(own_loss.shape, lambda i: (0, 0)),
            pl.BlockSpec((half, width), lambda i: (0, 0)),
            pl.BlockSpec((half, width), lambda i: (0, 0)),
            pl.BlockSpec((CHUNK, width), lambda i: (i, 0)),
        ],
        out_specs=[
            pl.BlockSpec((half, width), lambda i: (0, 0)),
            pl.BlockSpec((half, width), lambda i: (0, 0)),
            pl.BlockSpec((count, width + LANES), lambda i: (0, 0)),
        ],
        out_shape=[
            jax.ShapeDtypeStruct((half, width), jnp.float32),
            jax.ShapeDtypeStruct((half, width), jnp.float32),
            jax.ShapeDtypeStruct((count, width + LANES), jnp.bfloat16),
        ],
        scratch_shapes=[pltpu.VMEM((1, CHUNK), jnp.float32)],
        compiler_params=pltpu.CompilerParams(vmem_limit_bytes=LIMIT),
        cost_estimate=pl.CostEstimate(
            flops=12 * half * count * width, bytes_accessed=16 * half * width, transcendentals=6 * half * count
        ),
    )(place, heat_exponent, offset_added, own_loss, near, far, texts)


def grad_kernel(heat_ref, offset_ref, picture_ref, caption_ref, image_sum_ref, text_sum_ref, image_ref, text_ref):
    image_unit, image_norm = normalize(picture_ref[...])
    text_unit, text_norm = normalize(caption_ref[...])
    image_low, text_low = low(image_unit), low(text_unit)
    heat = jnp.exp(jnp.full((1, 1), heat_ref[0], jnp.float32))
    _, sigmoid = loss_and_sigmoid(-own_pairs(image_low, text_low, heat, offset_ref[0]))
    weights = low(-sigmoid * heat)
    image_ref[...] = back_norm(image_unit, image_norm, image_sum_ref[...] + weights * text_low)
    text_ref[...] = back_norm(text_unit, text_norm, text_sum_ref[...] + weights * image_low)


def gradients(heat_exponent, offset_added, pictures, captions, image_sum, text_sum):
    return pl.pallas_call(
        grad_kernel,
        in_specs=[pl.BlockSpec(memory_space=pltpu.SMEM)] * 2 + [pl.BlockSpec(memory_space=pltpu.VMEM)] * 4,
        out_shape=[jax.ShapeDtypeStruct(pictures.shape, jnp.float32)] * 2,
    )(heat_exponent, offset_added, pictures, captions, image_sum, text_sum)


def swapped(value, axis, step):
    return lax.ppermute(value, axis, [(i, i ^ step) for i in range(lax.axis_size(axis))])


def doubled(value, axis, step):
    return jnp.concatenate([value, swapped(value, axis, step)], axis=0)


def halved(value, axis, step):
    half = value.shape[0] // 2
    sent = (value[half:] * HALF).astype(jnp.float16)
    return value[:half] + swapped(sent, axis, step).astype(jnp.float32) * (1 / HALF)


def shards(picture_vectors, caption_vectors, heat_exponent, offset_added):
    rows, width = picture_vectors.shape
    plane, column = lax.axis_size(PLANE), lax.axis_size(COLUMN)
    steps = [1 << bit for bit in range(lax.axis_size("zl").bit_length() - 1)]
    image_low, text_low, own_loss = unit_rows(heat_exponent, offset_added, picture_vectors, caption_vectors)

    texts = doubled(text_low, "zh", 1)
    texts = lax.all_to_all(jnp.broadcast_to(texts[None], (plane, *texts.shape)), PLANE, 0, 0)
    near = image_low
    for step in reversed(steps):
        near = doubled(near, "zl", step)
    far = swapped(near, "c", 1)

    place = (lax.axis_index(PLANE) * 2 * rows).astype(jnp.int32).reshape(1)
    near_part, far_part, text_part = pair_terms(
        place, heat_exponent, offset_added, own_loss, near, far, texts.reshape(plane * 2 * rows, width)
    )

    text_parts = lax.all_to_all(text_part.reshape(plane, 2 * rows, width + LANES), PLANE, 0, 0)
    image_sum = near_part + swapped(far_part, "c", 1)
    for step in steps:
        image_sum = halved(image_sum, "zl", step)
    text_sum = halved(jnp.sum(text_parts[:, :, :width].astype(jnp.float32), axis=0), "zh", 1)

    plane_loss = jnp.sum(text_parts[:, 0, width : width + 3].astype(jnp.float32))
    losses = lax.all_to_all(jnp.broadcast_to(plane_loss, (column, 8, LANES)), COLUMN, 0, 0)
    loss_mean = (jnp.sum(losses[:, 0, 0]) / (rows * lax.axis_size(AXES))).reshape(1)
    image_grads, text_grads = gradients(
        heat_exponent, offset_added, picture_vectors, caption_vectors, image_sum, text_sum
    )
    return (loss_mean, image_grads, text_grads)


def solution(mesh):
    fine = Mesh(mesh.devices.reshape(SIZES), AXES)
    in_specs = (P(AXES, None), P(AXES, None), P(), P())
    out_specs = (P(), P(AXES, None), P(AXES, None))
    return jax.shard_map(shards, mesh=fine, in_specs=in_specs, out_specs=out_specs, check_vma=False)
```

```python
import jax
import jax.numpy as jnp
from jax import lax
from jax.experimental import pallas as pl
from jax.experimental.pallas import tpu as pltpu
from jax.sharding import Mesh, PartitionSpec as P

epsilon = 1e-06
AXES = ("zl", "x", "c", "y", "zh")
SIZES = (8, 4, 2, 4, 2)
PLANE = ("x", "y")
COLUMN = ("zl", "c", "zh")
LANES = 128
LIMIT = 20 * 1024 * 1024
HALF = 0.5


def normalize(raw_rows):
    row_norm = jnp.sqrt(jnp.sum(raw_rows * raw_rows, axis=1, keepdims=True) + epsilon)
    return (raw_rows / row_norm, row_norm)


def back_norm(unit_rows, row_norm, gradient):
    return (gradient - unit_rows * jnp.sum(unit_rows * gradient, axis=1, keepdims=True)) / row_norm


def low(rows):
    return rows.astype(jnp.bfloat16).astype(jnp.float32)


def loss_and_sigmoid(values):
    small = jnp.exp(-jnp.abs(values))
    loss = jnp.maximum(values, 0.0) + jnp.log1p(small)
    return loss, jnp.where(values >= 0, 1.0, small) / (1.0 + small)


def own_pairs(image_low, text_low, heat, offset):
    return jnp.sum(image_low * text_low, axis=1, keepdims=True) * heat + offset


def unit_kernel(heat_ref, offset_ref, picture_ref, caption_ref, image_ref, text_ref, loss_ref):
    image_unit, _ = normalize(picture_ref[...])
    text_unit, _ = normalize(caption_ref[...])
    image_low, text_low = image_unit.astype(jnp.bfloat16), text_unit.astype(jnp.bfloat16)
    image_ref[...] = image_low
    text_ref[...] = text_low
    heat = jnp.exp(jnp.full((1, 1), heat_ref[0], jnp.float32))
    logits = own_pairs(image_low.astype(jnp.float32), text_low.astype(jnp.float32), heat, offset_ref[0])
    loss, _ = loss_and_sigmoid(-logits)
    loss_ref[...] = loss


def unit_rows(heat_exponent, offset_added, pictures, captions):
    rows = pictures.shape[0]
    return pl.pallas_call(
        unit_kernel,
        in_specs=[pl.BlockSpec(memory_space=pltpu.SMEM)] * 2 + [pl.BlockSpec(memory_space=pltpu.VMEM)] * 2,
        out_shape=[
            jax.ShapeDtypeStruct(pictures.shape, jnp.bfloat16),
            jax.ShapeDtypeStruct(captions.shape, jnp.bfloat16),
            jax.ShapeDtypeStruct((rows, 1), jnp.float32),
        ],
    )(heat_exponent, offset_added, pictures, captions)


def pieces(total, shape):
    first = low(total)
    second = low(total - first)
    third = total - first - second
    lane = lax.broadcasted_iota(jnp.int32, shape, len(shape) - 1)
    spread = jnp.where(lane == 0, first, jnp.where(lane == 1, second, jnp.where(lane == 2, third, 0.0)))
    return spread.astype(jnp.bfloat16)


def pair_kernel(
    place_ref, heat_ref, offset_ref, own_loss_ref, near_ref, far_ref, own_ref, other_ref,
    near_out_ref, far_out_ref, own_out_ref, other_out_ref, loss_ref,
):
    rows = own_loss_ref.shape[0]
    heat = jnp.exp(jnp.full((1, 1), heat_ref[0], jnp.float32))
    total = jnp.sum(own_loss_ref[...], axis=0, keepdims=True)
    for text_ref, text_out_ref in ((own_ref, own_out_ref), (other_ref, other_out_ref)):
        texts = text_ref[...]
        text_part = None
        for image_ref, image_out_ref in ((near_ref, near_out_ref), (far_ref, far_out_ref)):
            images = image_ref[...]
            logits = lax.dot_general(
                images, texts, (((1,), (1,)), ((), ())), preferred_element_type=jnp.float32
            )
            logits = logits * heat + offset_ref[0]
            loss, sigmoid = loss_and_sigmoid(logits)
            weights = heat * sigmoid
            if image_ref is near_ref and text_ref is own_ref:
                image_row = lax.broadcasted_iota(jnp.int32, logits.shape, 0)
                text_row = lax.broadcasted_iota(jnp.int32, logits.shape, 1) - place_ref[0]
                match = (image_row == text_row) & (image_row < rows)
                weights = jnp.where(match, 0.0, weights)
                loss = jnp.where(match, 0.0, loss)
            weights = weights.astype(jnp.bfloat16)
            total += jnp.sum(jnp.sum(loss, axis=0, keepdims=True), axis=1, keepdims=True)
            image_part = jnp.dot(weights, texts, preferred_element_type=jnp.float32)
            part = lax.dot_general(
                weights, images, (((0,), (0,)), ((), ())), preferred_element_type=jnp.float32
            )
            text_part = part if text_part is None else text_part + part
            if text_ref is own_ref:
                image_out_ref[...] = image_part
            else:
                image_out_ref[...] += image_part
        text_out_ref[...] = text_part.astype(jnp.bfloat16)
    loss_ref[...] = jnp.broadcast_to(total, loss_ref.shape)


def pair_terms(place, heat_exponent, offset_added, own_loss, near, far, own, other):
    half, width = near.shape
    count = own.shape[0]
    return pl.pallas_call(
        pair_kernel,
        in_specs=[pl.BlockSpec(memory_space=pltpu.SMEM)] * 3 + [pl.BlockSpec(memory_space=pltpu.VMEM)] * 5,
        out_shape=[
            jax.ShapeDtypeStruct((half, width), jnp.float32),
            jax.ShapeDtypeStruct((half, width), jnp.float32),
            jax.ShapeDtypeStruct((count, width), jnp.bfloat16),
            jax.ShapeDtypeStruct((count, width), jnp.bfloat16),
            jax.ShapeDtypeStruct((8, LANES), jnp.float32),
        ],
        compiler_params=pltpu.CompilerParams(vmem_limit_bytes=LIMIT),
        cost_estimate=pl.CostEstimate(
            flops=24 * half * count * width, bytes_accessed=24 * half * width, transcendentals=12 * half * count
        ),
    )(place, heat_exponent, offset_added, own_loss, near, far, own, other)


def grad_kernel(heat_ref, offset_ref, picture_ref, caption_ref, image_sum_ref, text_sum_ref, image_ref, text_ref):
    image_unit, image_norm = normalize(picture_ref[...])
    text_unit, text_norm = normalize(caption_ref[...])
    image_low, text_low = low(image_unit), low(text_unit)
    heat = jnp.exp(jnp.full((1, 1), heat_ref[0], jnp.float32))
    _, sigmoid = loss_and_sigmoid(-own_pairs(image_low, text_low, heat, offset_ref[0]))
    weights = low(-sigmoid * heat)
    image_ref[...] = back_norm(image_unit, image_norm, image_sum_ref[...] + weights * text_low)
    text_ref[...] = back_norm(text_unit, text_norm, text_sum_ref[...] + weights * image_low)


def gradients(heat_exponent, offset_added, pictures, captions, image_sum, text_sum):
    return pl.pallas_call(
        grad_kernel,
        in_specs=[pl.BlockSpec(memory_space=pltpu.SMEM)] * 2 + [pl.BlockSpec(memory_space=pltpu.VMEM)] * 4,
        out_shape=[jax.ShapeDtypeStruct(pictures.shape, jnp.float32)] * 2,
    )(heat_exponent, offset_added, pictures, captions, image_sum, text_sum)


def swapped(value, axis, step):
    return lax.ppermute(value, axis, [(i, i ^ step) for i in range(lax.axis_size(axis))])


def doubled(value, axis, step):
    return jnp.concatenate([value, swapped(value, axis, step)], axis=0)


def halved(value, axis, step):
    half = value.shape[0] // 2
    sent = (value[half:] * HALF).astype(jnp.float16)
    return value[:half] + swapped(sent, axis, step).astype(jnp.float32) * (1 / HALF)


def gathered(block, axes):
    count = lax.axis_size(axes)
    parts = lax.all_to_all(jnp.broadcast_to(block[None], (count, *block.shape)), axes, 0, 0)
    return parts.reshape(count * block.shape[0], *block.shape[1:])


def shards(picture_vectors, caption_vectors, heat_exponent, offset_added):
    rows, width = picture_vectors.shape
    plane, column = lax.axis_size(PLANE), lax.axis_size(COLUMN)
    steps = [1 << bit for bit in range(lax.axis_size("zl").bit_length() - 1)]
    image_low, text_low, own_loss = unit_rows(heat_exponent, offset_added, picture_vectors, caption_vectors)

    own = gathered(text_low, PLANE)
    other = gathered(swapped(text_low, "zh", 1), PLANE)
    near = image_low
    for step in reversed(steps):
        near = doubled(near, "zl", step)
    far = swapped(near, "c", 1)

    place = (lax.axis_index(PLANE) * rows).astype(jnp.int32).reshape(1)
    near_part, far_part, own_part, other_part, loss = pair_terms(
        place, heat_exponent, offset_added, own_loss, near, far, own, other
    )

    other_parts = lax.all_to_all(other_part.reshape(plane, rows, width), PLANE, 0, 0)
    losses = lax.all_to_all(jnp.broadcast_to(loss[None], (column, *loss.shape)), COLUMN, 0, 0)
    column_loss = pieces(jnp.sum(losses[:, 0, 0]), (plane, rows, LANES))
    own_parts = lax.all_to_all(
        jnp.concatenate([own_part.reshape(plane, rows, width), column_loss], axis=2), PLANE, 0, 0
    )
    image_sum = near_part + swapped(far_part, "c", 1)
    for step in steps:
        image_sum = halved(image_sum, "zl", step)
    other_sum = jnp.sum(other_parts.astype(jnp.float32), axis=0)
    own_sum = jnp.sum(own_parts[:, :, :width].astype(jnp.float32), axis=0)
    text_sum = halved(jnp.concatenate([own_sum, other_sum], axis=0), "zh", 1)

    total_loss = jnp.sum(own_parts[:, 0, width : width + 3].astype(jnp.float32))
    loss_mean = (total_loss / (rows * lax.axis_size(AXES))).reshape(1)
    image_grads, text_grads = gradients(
        heat_exponent, offset_added, picture_vectors, caption_vectors, image_sum, text_sum
    )
    return (loss_mean, image_grads, text_grads)


def solution(mesh):
    fine = Mesh(mesh.devices.reshape(SIZES), AXES)
    in_specs = (P(AXES, None), P(AXES, None), P(), P())
    out_specs = (P(), P(AXES, None), P(AXES, None))
    return jax.shard_map(shards, mesh=fine, in_specs=in_specs, out_specs=out_specs, check_vma=False)
```

```python
import jax
import jax.numpy as jnp
from jax import lax
from jax.experimental import pallas as pl
from jax.experimental.pallas import tpu as pltpu
from jax.sharding import Mesh, PartitionSpec as P

epsilon = 1e-06
AXES = ("zl", "x", "c", "y", "zh")
SIZES = (8, 4, 2, 4, 2)
RING = ("zl", "zh")
PLANE = ("x", "y")
COLUMN = ("zl", "c", "zh")
LANES = 128
PARTS = 1
LIMIT = 20 * 1024 * 1024
HALF = 0.5


def normalize(raw_rows):
    row_norm = jnp.sqrt(jnp.sum(raw_rows * raw_rows, axis=1, keepdims=True) + epsilon)
    return (raw_rows / row_norm, row_norm)


def back_norm(unit_rows, row_norm, gradient):
    return (gradient - unit_rows * jnp.sum(unit_rows * gradient, axis=1, keepdims=True)) / row_norm


def low(rows):
    return rows.astype(jnp.bfloat16).astype(jnp.float32)


def loss_and_sigmoid(values):
    small = jnp.exp(-jnp.abs(values))
    loss = jnp.maximum(values, 0.0) + jnp.log1p(small)
    return loss, jnp.where(values >= 0, 1.0, small) / (1.0 + small)


def own_pairs(image_low, text_low, heat, offset):
    return jnp.sum(image_low * text_low, axis=1, keepdims=True) * heat + offset


def unit_kernel(heat_ref, offset_ref, picture_ref, caption_ref, image_ref, text_ref, loss_ref):
    image_unit, _ = normalize(picture_ref[...])
    text_unit, _ = normalize(caption_ref[...])
    image_low, text_low = image_unit.astype(jnp.bfloat16), text_unit.astype(jnp.bfloat16)
    image_ref[...] = image_low
    text_ref[...] = text_low
    heat = jnp.exp(jnp.full((1, 1), heat_ref[0], jnp.float32))
    logits = own_pairs(image_low.astype(jnp.float32), text_low.astype(jnp.float32), heat, offset_ref[0])
    loss, _ = loss_and_sigmoid(-logits)
    loss_ref[...] = loss


def unit_rows(heat_exponent, offset_added, pictures, captions):
    rows = pictures.shape[0]
    return pl.pallas_call(
        unit_kernel,
        in_specs=[pl.BlockSpec(memory_space=pltpu.SMEM)] * 2 + [pl.BlockSpec(memory_space=pltpu.VMEM)] * 2,
        out_shape=[
            jax.ShapeDtypeStruct(pictures.shape, jnp.bfloat16),
            jax.ShapeDtypeStruct(captions.shape, jnp.bfloat16),
            jax.ShapeDtypeStruct((rows, 1), jnp.float32),
        ],
    )(heat_exponent, offset_added, pictures, captions)


def pieces(total, shape):
    first = low(total)
    second = low(total - first)
    third = total - first - second
    lane = lax.broadcasted_iota(jnp.int32, shape, len(shape) - 1)
    spread = jnp.where(lane == 0, first, jnp.where(lane == 1, second, jnp.where(lane == 2, third, 0.0)))
    return spread.astype(jnp.bfloat16)


def pair_kernel(place_ref, heat_ref, offset_ref, own_loss_ref, near_ref, far_ref, text_ref, weight_ref, text_out_ref):
    rows = own_loss_ref.shape[0]
    half, width = near_ref.shape
    count = text_ref.shape[0] // PARTS
    heat = jnp.exp(jnp.full((1, 1), heat_ref[0], jnp.float32))
    total = jnp.sum(own_loss_ref[...], axis=0, keepdims=True)
    for part in range(PARTS):
        columns = slice(part * count, (part + 1) * count)
        texts = text_ref[columns]
        text_part = None
        for place, image_ref in enumerate((near_ref, far_ref)):
            images = image_ref[...]
            logits = lax.dot_general(
                images, texts, (((1,), (1,)), ((), ())), preferred_element_type=jnp.float32
            )
            logits = logits * heat + offset_ref[0]
            loss, sigmoid = loss_and_sigmoid(logits)
            weights = heat * sigmoid
            if image_ref is near_ref:
                image_row = lax.broadcasted_iota(jnp.int32, logits.shape, 0) - rows
                text_row = lax.broadcasted_iota(jnp.int32, logits.shape, 1) + (part * count - place_ref[0])
                match = (image_row == text_row) & (image_row >= 0) & (image_row < rows)
                weights = jnp.where(match, 0.0, weights)
                loss = jnp.where(match, 0.0, loss)
            weights = weights.astype(jnp.bfloat16)
            weight_ref[place * half : (place + 1) * half, columns] = weights
            total += jnp.sum(jnp.sum(loss, axis=0, keepdims=True), axis=1, keepdims=True)
            term = lax.dot_general(
                weights, images, (((0,), (0,)), ((), ())), preferred_element_type=jnp.float32
            )
            text_part = term if text_part is None else text_part + term
        text_out_ref[columns, :width] = text_part.astype(jnp.bfloat16)
    text_out_ref[:, width:] = pieces(total, (text_out_ref.shape[0], LANES))


def pair_terms(place, heat_exponent, offset_added, own_loss, near, far, texts):
    half, width = near.shape
    count = texts.shape[0]
    return pl.pallas_call(
        pair_kernel,
        in_specs=[pl.BlockSpec(memory_space=pltpu.SMEM)] * 3 + [pl.BlockSpec(memory_space=pltpu.VMEM)] * 4,
        out_shape=[
            jax.ShapeDtypeStruct((2 * half, count), jnp.bfloat16),
            jax.ShapeDtypeStruct((count, width + LANES), jnp.bfloat16),
        ],
        compiler_params=pltpu.CompilerParams(vmem_limit_bytes=LIMIT),
        cost_estimate=pl.CostEstimate(
            flops=8 * half * count * width, bytes_accessed=8 * half * width, transcendentals=6 * half * count
        ),
    )(place, heat_exponent, offset_added, own_loss, near, far, texts)


def image_kernel(weight_ref, text_ref, near_ref, far_ref):
    half = near_ref.shape[0]
    texts = text_ref[...]
    far_ref[...] = jnp.dot(weight_ref[half:], texts, preferred_element_type=jnp.float32)
    near_ref[...] = jnp.dot(weight_ref[:half], texts, preferred_element_type=jnp.float32)


def image_terms(weights, texts):
    half, width = weights.shape[0] // 2, texts.shape[1]
    return pl.pallas_call(
        image_kernel,
        in_specs=[pl.BlockSpec(memory_space=pltpu.VMEM)] * 2,
        out_shape=[jax.ShapeDtypeStruct((half, width), jnp.float32)] * 2,
        compiler_params=pltpu.CompilerParams(vmem_limit_bytes=LIMIT),
        cost_estimate=pl.CostEstimate(
            flops=4 * half * texts.shape[0] * width, bytes_accessed=16 * half * width, transcendentals=0
        ),
    )(weights, texts)


def grad_kernel(
    heat_ref, offset_ref, picture_ref, caption_ref, image_sum_ref, text_sum_ref, image_ref, text_ref
):
    image_unit, image_norm = normalize(picture_ref[...])
    text_unit, text_norm = normalize(caption_ref[...])
    image_low, text_low = low(image_unit), low(text_unit)
    heat = jnp.exp(jnp.full((1, 1), heat_ref[0], jnp.float32))
    _, sigmoid = loss_and_sigmoid(-own_pairs(image_low, text_low, heat, offset_ref[0]))
    weights = low(-sigmoid * heat)
    image_ref[...] = back_norm(image_unit, image_norm, image_sum_ref[...] + weights * text_low)
    text_ref[...] = back_norm(text_unit, text_norm, text_sum_ref[...] + weights * image_low)


def gradients(heat_exponent, offset_added, pictures, captions, image_sum, text_sum):
    return pl.pallas_call(
        grad_kernel,
        in_specs=[pl.BlockSpec(memory_space=pltpu.SMEM)] * 2 + [pl.BlockSpec(memory_space=pltpu.VMEM)] * 4,
        out_shape=[jax.ShapeDtypeStruct(pictures.shape, jnp.float32)] * 2,
    )(heat_exponent, offset_added, pictures, captions, image_sum, text_sum)


def moved(value, steps):
    halves = lax.axis_size("zh")
    count = lax.axis_size(RING)
    order = [low_place * halves + half for half in range(halves) for low_place in range(count // halves)]
    return lax.ppermute(value, RING, [(order[i], order[(i + steps) % count]) for i in range(count)])


def sent(value):
    return (value * HALF).astype(jnp.float16)


def received(value):
    return value.astype(jnp.float32) * (1 / HALF)


def swapped(value):
    return lax.ppermute(value, "c", [(0, 1), (1, 0)])


def ring_gathered(block, texts):
    rows = block.shape[0]
    same = jnp.concatenate([moved(block, 4), block, moved(block, -4), moved(block, 8)], axis=0)
    parts = [same, moved(same, -1), moved(same, 1)]
    parts += [moved(same[rows : 3 * rows], -2), moved(same[: 2 * rows], 2)]
    near = jnp.concatenate(parts, axis=0)
    return lax.optimization_barrier((near, texts))


def near_summed(value, rows):
    low_part = sent(value)
    up = received(moved(low_part[4 * rows : 8 * rows], 1))
    down = received(moved(low_part[8 * rows : 12 * rows], -1))
    up_two = received(moved(low_part[12 * rows : 14 * rows], 2))
    down_two = received(moved(low_part[14 * rows :], -2))
    same = value[: 4 * rows] + up + down
    own = same[rows : 2 * rows] + down_two[rows:] + up_two[:rows]
    others = (same[:rows] + down_two[:rows], same[2 * rows : 3 * rows] + up_two[rows:], same[3 * rows :])
    return own, [sent(other) for other in others]


def far_summed(own, others):
    for other, steps in zip(others, (-4, 4, 8)):
        own += received(moved(other, steps))
    return own


def shards(picture_vectors, caption_vectors, heat_exponent, offset_added):
    rows, width = picture_vectors.shape
    plane, column = lax.axis_size(PLANE), lax.axis_size(COLUMN)
    image_low, text_low, own_loss = unit_rows(heat_exponent, offset_added, picture_vectors, caption_vectors)

    texts = lax.all_to_all(jnp.broadcast_to(text_low[None], (plane, *text_low.shape)), PLANE, 0, 0)
    near, texts = ring_gathered(image_low, texts.reshape(plane * rows, width))
    far = swapped(near)

    place = (lax.axis_index(PLANE) * rows).astype(jnp.int32).reshape(1)
    weights, text_part = pair_terms(place, heat_exponent, offset_added, own_loss, near, far, texts)
    text_parts = lax.all_to_all(text_part.reshape(plane, rows, width + LANES), PLANE, 0, 0)
    near_part, far_part = image_terms(weights, texts)
    own, others = near_summed(near_part + swapped(far_part), rows)
    others, text_parts = lax.optimization_barrier((others, text_parts))
    plane_loss = jnp.sum(text_parts[:, 0, width : width + 3].astype(jnp.float32))
    losses = lax.all_to_all(jnp.broadcast_to(plane_loss, (column, 8, LANES)), COLUMN, 0, 0)
    loss_mean = (jnp.sum(losses[:, 0, 0]) / (rows * lax.axis_size(AXES))).reshape(1)
    text_sum = jnp.sum(text_parts[:, :, :width].astype(jnp.float32), axis=0)
    image_sum = far_summed(own, others)
    image_grads, text_grads = gradients(
        heat_exponent, offset_added, picture_vectors, caption_vectors, image_sum, text_sum
    )
    return (loss_mean, image_grads, text_grads)


def solution(mesh):
    fine = Mesh(mesh.devices.reshape(SIZES), AXES)
    in_specs = (P(AXES, None), P(AXES, None), P(), P())
    out_specs = (P(), P(AXES, None), P(AXES, None))
    return jax.shard_map(shards, mesh=fine, in_specs=in_specs, out_specs=out_specs, check_vma=False)
```

```python
import jax
import jax.numpy as jnp
from jax import lax
from jax.experimental import pallas as pl
from jax.experimental.pallas import tpu as pltpu
from jax.sharding import Mesh, PartitionSpec as P

epsilon = 1e-06
AXES = ("zl", "x", "c", "y", "zh")
SIZES = (8, 4, 2, 4, 2)
RING = ("zl", "zh")
PLANE = ("x", "y")
LANES = 128
PARTS = 1
LIMIT = 20 * 1024 * 1024
HALF = 0.5


def normalize(raw_rows):
    row_norm = jnp.sqrt(jnp.sum(raw_rows * raw_rows, axis=1, keepdims=True) + epsilon)
    return (raw_rows / row_norm, row_norm)


def back_norm(unit_rows, row_norm, gradient):
    return (gradient - unit_rows * jnp.sum(unit_rows * gradient, axis=1, keepdims=True)) / row_norm


def low(rows):
    return rows.astype(jnp.bfloat16).astype(jnp.float32)


def loss_and_sigmoid(values):
    small = jnp.exp(-jnp.abs(values))
    loss = jnp.maximum(values, 0.0) + jnp.log1p(small)
    return loss, jnp.where(values >= 0, 1.0, small) / (1.0 + small)


def own_pairs(image_low, text_low, heat, offset):
    return jnp.sum(image_low * text_low, axis=1, keepdims=True) * heat + offset


def unit_kernel(heat_ref, offset_ref, picture_ref, caption_ref, image_ref, text_ref, loss_ref):
    image_unit, _ = normalize(picture_ref[...])
    text_unit, _ = normalize(caption_ref[...])
    image_low, text_low = image_unit.astype(jnp.bfloat16), text_unit.astype(jnp.bfloat16)
    image_ref[...] = image_low
    text_ref[...] = jnp.broadcast_to(text_low[None], text_ref.shape)
    heat = jnp.exp(jnp.full((1, 1), heat_ref[0], jnp.float32))
    logits = own_pairs(image_low.astype(jnp.float32), text_low.astype(jnp.float32), heat, offset_ref[0])
    loss, _ = loss_and_sigmoid(-logits)
    loss_ref[...] = loss


def unit_rows(copies, heat_exponent, offset_added, pictures, captions):
    rows = pictures.shape[0]
    return pl.pallas_call(
        unit_kernel,
        in_specs=[pl.BlockSpec(memory_space=pltpu.SMEM)] * 2 + [pl.BlockSpec(memory_space=pltpu.VMEM)] * 2,
        out_shape=[
            jax.ShapeDtypeStruct(pictures.shape, jnp.bfloat16),
            jax.ShapeDtypeStruct((copies, *captions.shape), jnp.bfloat16),
            jax.ShapeDtypeStruct((rows, 1), jnp.float32),
        ],
    )(heat_exponent, offset_added, pictures, captions)


def pieces(total, shape):
    first = low(total)
    second = low(total - first)
    third = total - first - second
    lane = lax.broadcasted_iota(jnp.int32, shape, len(shape) - 1)
    spread = jnp.where(lane == 0, first, jnp.where(lane == 1, second, jnp.where(lane == 2, third, 0.0)))
    return spread.astype(jnp.bfloat16)


def pair_kernel(place_ref, heat_ref, offset_ref, own_loss_ref, near_ref, far_ref, text_ref, weight_ref, text_out_ref):
    rows = own_loss_ref.shape[0]
    half, width = near_ref.shape
    count = text_ref.shape[0] // PARTS
    heat = jnp.exp(jnp.full((1, 1), heat_ref[0], jnp.float32))
    total = jnp.sum(own_loss_ref[...], axis=0, keepdims=True)
    for part in range(PARTS):
        columns = slice(part * count, (part + 1) * count)
        texts = text_ref[columns]
        text_part = None
        for place, image_ref in enumerate((near_ref, far_ref)):
            images = image_ref[...]
            logits = lax.dot_general(
                images, texts, (((1,), (1,)), ((), ())), preferred_element_type=jnp.float32
            )
            logits = logits * heat + offset_ref[0]
            loss, sigmoid = loss_and_sigmoid(logits)
            weights = heat * sigmoid
            if image_ref is near_ref:
                image_row = lax.broadcasted_iota(jnp.int32, logits.shape, 0) - rows
                text_row = lax.broadcasted_iota(jnp.int32, logits.shape, 1) + (part * count - place_ref[0])
                match = (image_row == text_row) & (image_row >= 0) & (image_row < rows)
                weights = jnp.where(match, 0.0, weights)
                loss = jnp.where(match, 0.0, loss)
            weights = weights.astype(jnp.bfloat16)
            weight_ref[place * half : (place + 1) * half, columns] = weights
            total += jnp.sum(jnp.sum(loss, axis=0, keepdims=True), axis=1, keepdims=True)
            term = lax.dot_general(
                weights, images, (((0,), (0,)), ((), ())), preferred_element_type=jnp.float32
            )
            text_part = term if text_part is None else text_part + term
        text_out_ref[columns, :width] = text_part.astype(jnp.bfloat16)
    text_out_ref[:, width:] = pieces(total, (text_out_ref.shape[0], LANES))


def pair_terms(place, heat_exponent, offset_added, own_loss, near, far, texts):
    half, width = near.shape
    count = texts.shape[0]
    return pl.pallas_call(
        pair_kernel,
        in_specs=[pl.BlockSpec(memory_space=pltpu.SMEM)] * 3 + [pl.BlockSpec(memory_space=pltpu.VMEM)] * 4,
        out_shape=[
            jax.ShapeDtypeStruct((2 * half, count), jnp.bfloat16),
            jax.ShapeDtypeStruct((count, width + LANES), jnp.bfloat16),
        ],
        compiler_params=pltpu.CompilerParams(vmem_limit_bytes=LIMIT),
        cost_estimate=pl.CostEstimate(
            flops=8 * half * count * width, bytes_accessed=8 * half * width, transcendentals=6 * half * count
        ),
    )(place, heat_exponent, offset_added, own_loss, near, far, texts)


def image_kernel(weight_ref, text_ref, near_ref, far_ref):
    half = near_ref.shape[0]
    texts = text_ref[...]
    far_ref[...] = jnp.dot(weight_ref[half:], texts, preferred_element_type=jnp.float32)
    near_ref[...] = jnp.dot(weight_ref[:half], texts, preferred_element_type=jnp.float32)


def image_terms(weights, texts):
    half, width = weights.shape[0] // 2, texts.shape[1]
    return pl.pallas_call(
        image_kernel,
        in_specs=[pl.BlockSpec(memory_space=pltpu.VMEM)] * 2,
        out_shape=[jax.ShapeDtypeStruct((half, width), jnp.float32)] * 2,
        compiler_params=pltpu.CompilerParams(vmem_limit_bytes=LIMIT),
        cost_estimate=pl.CostEstimate(
            flops=4 * half * texts.shape[0] * width, bytes_accessed=16 * half * width, transcendentals=0
        ),
    )(weights, texts)


def grad_kernel(
    heat_ref, offset_ref, picture_ref, caption_ref, image_sum_ref, text_sum_ref, image_ref, text_ref
):
    image_unit, image_norm = normalize(picture_ref[...])
    text_unit, text_norm = normalize(caption_ref[...])
    image_low, text_low = low(image_unit), low(text_unit)
    heat = jnp.exp(jnp.full((1, 1), heat_ref[0], jnp.float32))
    _, sigmoid = loss_and_sigmoid(-own_pairs(image_low, text_low, heat, offset_ref[0]))
    weights = low(-sigmoid * heat)
    image_ref[...] = back_norm(image_unit, image_norm, image_sum_ref[...] + weights * text_low)
    text_ref[...] = back_norm(text_unit, text_norm, text_sum_ref[...] + weights * image_low)


def gradients(heat_exponent, offset_added, pictures, captions, image_sum, text_sum):
    return pl.pallas_call(
        grad_kernel,
        in_specs=[pl.BlockSpec(memory_space=pltpu.SMEM)] * 2 + [pl.BlockSpec(memory_space=pltpu.VMEM)] * 4,
        out_shape=[jax.ShapeDtypeStruct(pictures.shape, jnp.float32)] * 2,
    )(heat_exponent, offset_added, pictures, captions, image_sum, text_sum)


def moved(value, steps):
    halves = lax.axis_size("zh")
    count = lax.axis_size(RING)
    order = [low_place * halves + half for half in range(halves) for low_place in range(count // halves)]
    return lax.ppermute(value, RING, [(order[i], order[(i + steps) % count]) for i in range(count)])


def sent(value):
    return (value * HALF).astype(jnp.float16)


def received(value):
    return value.astype(jnp.float32) * (1 / HALF)


def swapped(value):
    return lax.ppermute(value, "c", [(0, 1), (1, 0)])


def ring_gathered(block, texts):
    rows = block.shape[0]
    same = jnp.concatenate([moved(block, 4), block, moved(block, -4), moved(block, 8)], axis=0)
    parts = [same, moved(same, -1), moved(same, 1)]
    parts += [moved(same[rows : 3 * rows], -2), moved(same[: 2 * rows], 2)]
    near = jnp.concatenate(parts, axis=0)
    return lax.optimization_barrier((near, texts))


LOSS_SCALE = 2.0**-15
REST_SCALE = 2.0**11


def with_loss(value, loss):
    scaled = loss * LOSS_SCALE
    first = scaled.astype(jnp.float16)
    rest = ((scaled - first.astype(jnp.float32)) * REST_SCALE).astype(jnp.float16)
    return jnp.concatenate([sent(value), first, rest], axis=0)


def loss_of(arrived):
    first, rest = arrived[-8:-4].astype(jnp.float32), arrived[-4:].astype(jnp.float32)
    return (first + rest * (1 / REST_SCALE)) * (1 / LOSS_SCALE)


def near_summed(value, rows, loss):
    up = moved(with_loss(value[4 * rows : 8 * rows], loss), 1)
    down = moved(with_loss(value[8 * rows : 12 * rows], loss), -1)
    up_two = moved(with_loss(value[12 * rows : 14 * rows], loss), 2)
    down_two = received(moved(sent(value[14 * rows :]), -2))
    loss = loss + loss_of(up) + loss_of(down) + loss_of(up_two)
    same = value[: 4 * rows] + received(up[:-8]) + received(down[:-8])
    up_two = received(up_two[:-8])
    own = same[rows : 2 * rows] + down_two[rows:] + up_two[:rows]
    others = (same[:rows] + down_two[:rows], same[2 * rows : 3 * rows] + up_two[rows:], same[3 * rows :])
    return own, others, loss


def far_summed(own, others, loss):
    arrived = [moved(with_loss(other, loss), steps) for other, steps in zip(others, (-4, 4, 8))]
    for part in arrived:
        own = own + received(part[:-8])
        loss = loss + loss_of(part)
    return own, loss


def shards(picture_vectors, caption_vectors, heat_exponent, offset_added):
    rows, width = picture_vectors.shape
    plane = lax.axis_size(PLANE)
    image_low, text_low, own_loss = unit_rows(plane, heat_exponent, offset_added, picture_vectors, caption_vectors)

    texts = lax.all_to_all(text_low, PLANE, 0, 0).reshape(plane * rows, width)
    near, texts = ring_gathered(image_low, texts)
    far = swapped(near)

    place = (lax.axis_index(PLANE) * rows).astype(jnp.int32).reshape(1)
    weights, text_part = pair_terms(place, heat_exponent, offset_added, own_loss, near, far, texts)
    text_parts = lax.all_to_all(text_part.reshape(plane, rows, width + LANES), PLANE, 0, 0)
    near_part, far_part = image_terms(weights, texts)
    image_part = near_part + swapped(far_part)
    loss = jnp.tile(jnp.sum(text_parts[:, :4, width:].astype(jnp.float32), axis=0), (1, width // LANES))
    text_sum = jnp.sum(text_parts[:, :, :width].astype(jnp.float32), axis=0)
    image_sum, loss = far_summed(*near_summed(image_part, rows, loss))
    loss = loss[:, :LANES]
    total = jnp.sum((loss + swapped(loss))[0, :3])
    loss_mean = (total / (rows * lax.axis_size(AXES))).reshape(1)
    image_grads, text_grads = gradients(
        heat_exponent, offset_added, picture_vectors, caption_vectors, image_sum, text_sum
    )
    return (loss_mean, image_grads, text_grads)


def solution(mesh):
    fine = Mesh(mesh.devices.reshape(SIZES), AXES)
    in_specs = (P(AXES, None), P(AXES, None), P(), P())
    out_specs = (P(), P(AXES, None), P(AXES, None))
    return jax.shard_map(shards, mesh=fine, in_specs=in_specs, out_specs=out_specs, check_vma=False)
```

```python
import jax
import jax.numpy as jnp
from jax import lax
from jax.experimental import pallas as pl
from jax.experimental.pallas import tpu as pltpu
from jax.sharding import Mesh, PartitionSpec as P

epsilon = 1e-06
AXES = ("zl", "x", "c", "y", "zh")
SIZES = (8, 4, 2, 4, 2)
PLANE = ("x", "y")
LANES = 128
LIMIT = 20 * 1024 * 1024
HALF = 0.5


def normalize(raw_rows):
    row_norm = jnp.sqrt(jnp.sum(raw_rows * raw_rows, axis=1, keepdims=True) + epsilon)
    return (raw_rows / row_norm, row_norm)


def back_norm(unit_rows, row_norm, gradient):
    return (gradient - unit_rows * jnp.sum(unit_rows * gradient, axis=1, keepdims=True)) / row_norm


def low(rows):
    return rows.astype(jnp.bfloat16).astype(jnp.float32)


def loss_and_sigmoid(values):
    small = jnp.exp(-jnp.abs(values))
    loss = jnp.maximum(values, 0.0) + jnp.log1p(small)
    return loss, jnp.where(values >= 0, 1.0, small) / (1.0 + small)


def own_pairs(image_low, text_low, heat, offset):
    return jnp.sum(image_low * text_low, axis=1, keepdims=True) * heat + offset


def unit_kernel(heat_ref, offset_ref, picture_ref, caption_ref, image_ref, text_ref, loss_ref):
    image_unit, _ = normalize(picture_ref[...])
    text_unit, _ = normalize(caption_ref[...])
    image_low, text_low = image_unit.astype(jnp.bfloat16), text_unit.astype(jnp.bfloat16)
    image_ref[...] = image_low
    text_ref[...] = text_low
    heat = jnp.exp(jnp.full((1, 1), heat_ref[0], jnp.float32))
    logits = own_pairs(image_low.astype(jnp.float32), text_low.astype(jnp.float32), heat, offset_ref[0])
    loss, _ = loss_and_sigmoid(-logits)
    loss_ref[...] = loss


def unit_rows(heat_exponent, offset_added, pictures, captions):
    rows = pictures.shape[0]
    return pl.pallas_call(
        unit_kernel,
        in_specs=[pl.BlockSpec(memory_space=pltpu.SMEM)] * 2 + [pl.BlockSpec(memory_space=pltpu.VMEM)] * 2,
        out_shape=[
            jax.ShapeDtypeStruct(pictures.shape, jnp.bfloat16),
            jax.ShapeDtypeStruct(captions.shape, jnp.bfloat16),
            jax.ShapeDtypeStruct((rows, 1), jnp.float32),
        ],
    )(heat_exponent, offset_added, pictures, captions)


def pair_kernel(place_ref, heat_ref, offset_ref, own_loss_ref, near_ref, far_ref, text_ref, weight_ref, loss_ref):
    rows = own_loss_ref.shape[0]
    half = near_ref.shape[0]
    texts = text_ref[...]
    heat = jnp.exp(jnp.full((1, 1), heat_ref[0], jnp.float32))
    total = jnp.sum(own_loss_ref[...], axis=0, keepdims=True)
    for place, image_ref in enumerate((near_ref, far_ref)):
        logits = lax.dot_general(
            image_ref[...], texts, (((1,), (1,)), ((), ())), preferred_element_type=jnp.float32
        )
        logits = logits * heat + offset_ref[0]
        loss, sigmoid = loss_and_sigmoid(logits)
        weights = heat * sigmoid
        if image_ref is near_ref:
            image_row = lax.broadcasted_iota(jnp.int32, logits.shape, 0)
            text_row = lax.broadcasted_iota(jnp.int32, logits.shape, 1) - place_ref[0]
            match = (image_row == text_row) & (image_row < rows)
            weights = jnp.where(match, 0.0, weights)
            loss = jnp.where(match, 0.0, loss)
        weight_ref[place * half : (place + 1) * half] = weights.astype(jnp.bfloat16)
        total += jnp.sum(jnp.sum(loss, axis=0, keepdims=True), axis=1, keepdims=True)
    loss_ref[...] = jnp.broadcast_to(total[None], loss_ref.shape)


def pair_weights(copies, place, heat_exponent, offset_added, own_loss, near, far, texts):
    half, width = near.shape
    count = texts.shape[0]
    return pl.pallas_call(
        pair_kernel,
        in_specs=[pl.BlockSpec(memory_space=pltpu.SMEM)] * 3 + [pl.BlockSpec(memory_space=pltpu.VMEM)] * 4,
        out_shape=[
            jax.ShapeDtypeStruct((2 * half, count), jnp.bfloat16),
            jax.ShapeDtypeStruct((copies, 8, LANES), jnp.float32),
        ],
        compiler_params=pltpu.CompilerParams(vmem_limit_bytes=LIMIT),
        cost_estimate=pl.CostEstimate(
            flops=4 * half * count * width, bytes_accessed=8 * half * width, transcendentals=6 * half * count
        ),
    )(place, heat_exponent, offset_added, own_loss, near, far, texts)


def terms_kernel(weight_ref, near_ref, far_ref, text_ref, near_out_ref, far_out_ref, own_out_ref, other_out_ref):
    half = near_ref.shape[0]
    rows = own_out_ref.shape[1]
    texts = text_ref[...]
    far_out_ref[...] = jnp.dot(weight_ref[half:], texts, preferred_element_type=jnp.float32)
    near_out_ref[...] = jnp.dot(weight_ref[:half], texts, preferred_element_type=jnp.float32)
    text_part = lax.dot_general(
        weight_ref[:half], near_ref[...], (((0,), (0,)), ((), ())), preferred_element_type=jnp.float32
    )
    text_part += lax.dot_general(
        weight_ref[half:], far_ref[...], (((0,), (0,)), ((), ())), preferred_element_type=jnp.float32
    )
    for place in range(own_out_ref.shape[0]):
        start = 2 * place * rows
        own_out_ref[place] = text_part[start : start + rows].astype(jnp.bfloat16)
        other_out_ref[place] = text_part[start + rows : start + 2 * rows].astype(jnp.bfloat16)


def pair_terms(copies, weights, near, far, texts):
    block = jax.ShapeDtypeStruct((copies, texts.shape[0] // copies // 2, texts.shape[1]), jnp.bfloat16)
    return pl.pallas_call(
        terms_kernel,
        in_specs=[pl.BlockSpec(memory_space=pltpu.VMEM)] * 4,
        out_shape=[
            jax.ShapeDtypeStruct(near.shape, jnp.float32),
            jax.ShapeDtypeStruct(far.shape, jnp.float32),
            block,
            block,
        ],
        compiler_params=pltpu.CompilerParams(vmem_limit_bytes=LIMIT),
        cost_estimate=pl.CostEstimate(
            flops=4 * weights.size * near.shape[1], bytes_accessed=16 * near.size, transcendentals=0
        ),
    )(weights, near, far, texts)


def grad_kernel(
    heat_ref, offset_ref, picture_ref, caption_ref, image_sum_ref, text_sum_ref, image_ref, text_ref
):
    image_unit, image_norm = normalize(picture_ref[...])
    text_unit, text_norm = normalize(caption_ref[...])
    image_low, text_low = low(image_unit), low(text_unit)
    heat = jnp.exp(jnp.full((1, 1), heat_ref[0], jnp.float32))
    _, sigmoid = loss_and_sigmoid(-own_pairs(image_low, text_low, heat, offset_ref[0]))
    weights = low(-sigmoid * heat)
    image_ref[...] = back_norm(image_unit, image_norm, image_sum_ref[...] + weights * text_low)
    text_ref[...] = back_norm(text_unit, text_norm, text_sum_ref[...] + weights * image_low)


def gradients(heat_exponent, offset_added, pictures, captions, image_sum, text_sum):
    return pl.pallas_call(
        grad_kernel,
        in_specs=[pl.BlockSpec(memory_space=pltpu.SMEM)] * 2 + [pl.BlockSpec(memory_space=pltpu.VMEM)] * 4,
        out_shape=[jax.ShapeDtypeStruct(pictures.shape, jnp.float32)] * 2,
    )(heat_exponent, offset_added, pictures, captions, image_sum, text_sum)


def swapped(value, axis, step):
    return lax.ppermute(value, axis, [(i, i ^ step) for i in range(lax.axis_size(axis))])


def doubled(value, axis, step):
    return jnp.concatenate([value, swapped(value, axis, step)], axis=0)


def sent(value):
    return (value * HALF).astype(jnp.float16)


def received(value):
    return value.astype(jnp.float32) * (1 / HALF)


LOSS_SCALE = 2.0**-15
REST_SCALE = 2.0**11


def halved(value, loss, axis, step):
    half, width = value.shape[0] // 2, value.shape[1]
    scaled = loss * LOSS_SCALE
    first = scaled.astype(jnp.float16)
    rest = ((scaled - first.astype(jnp.float32)) * REST_SCALE).astype(jnp.float16)
    tail = jnp.pad(jnp.concatenate([first, rest], axis=0), ((0, 0), (0, width - LANES)))
    arrived = swapped(jnp.concatenate([sent(value[half:]), tail], axis=0), axis, step)
    first, rest = arrived[half : half + 4, :LANES], arrived[half + 4 :, :LANES]
    loss = loss + (first.astype(jnp.float32) + rest.astype(jnp.float32) * (1 / REST_SCALE)) * (1 / LOSS_SCALE)
    return value[:half] + received(arrived[:half]), loss


def shards(picture_vectors, caption_vectors, heat_exponent, offset_added):
    rows, width = picture_vectors.shape
    plane = lax.axis_size(PLANE)
    steps = [1 << bit for bit in range(lax.axis_size("zl").bit_length() - 1)]
    image_low, text_low, own_loss = unit_rows(heat_exponent, offset_added, picture_vectors, caption_vectors)

    other_low = swapped(text_low, "zh", 1)
    copies = [jnp.broadcast_to(part[None], (plane, rows, width)) for part in (text_low, other_low)]
    texts = lax.all_to_all(jnp.concatenate(copies, axis=1), PLANE, 0, 0)
    texts = texts.reshape(plane * 2 * rows, width)
    near = image_low
    for step in reversed(steps):
        near = doubled(near, "zl", step)
    far = swapped(near, "c", 1)

    place = (lax.axis_index(PLANE) * 2 * rows).astype(jnp.int32).reshape(1)
    weights, loss = pair_weights(plane, place, heat_exponent, offset_added, own_loss, near, far, texts)
    loss = jnp.sum(lax.all_to_all(loss, PLANE, 0, 0)[:, :4], axis=0)
    near_part, far_part, own_part, other_part = pair_terms(plane, weights, near, far, texts)
    other_parts = lax.all_to_all(other_part, PLANE, 0, 0)
    own_parts = lax.all_to_all(own_part, PLANE, 0, 0)

    image_sum = near_part + swapped(far_part, "c", 1)
    for step in steps:
        image_sum, loss = halved(image_sum, loss, "zl", step)
    loss += swapped(loss, "zh", 1)
    total = (loss + swapped(loss, "c", 1))[0, 0]
    loss_mean = (total / (rows * lax.axis_size(AXES))).reshape(1)
    other_sum = jnp.sum(other_parts.astype(jnp.float32), axis=0)
    text_sum = received(swapped(sent(other_sum), "zh", 1)) + jnp.sum(own_parts.astype(jnp.float32), axis=0)
    image_grads, text_grads = gradients(
        heat_exponent, offset_added, picture_vectors, caption_vectors, image_sum, text_sum
    )
    return (loss_mean, image_grads, text_grads)


def solution(mesh):
    fine = Mesh(mesh.devices.reshape(SIZES), AXES)
    in_specs = (P(AXES, None), P(AXES, None), P(), P())
    out_specs = (P(), P(AXES, None), P(AXES, None))
    return jax.shard_map(shards, mesh=fine, in_specs=in_specs, out_specs=out_specs, check_vma=False)
```

```python
import jax
import jax.numpy as jnp
from jax import lax
from jax.experimental import pallas as pl
from jax.experimental.pallas import tpu as pltpu
from jax.sharding import Mesh, PartitionSpec as P

epsilon = 1e-06
AXES = ("zl", "xh", "xl", "c", "y", "zh")
SIZES = (8, 2, 2, 2, 4, 2)
PLANE = ("xh", "y")
COLUMN = ("zl", "xl", "c", "zh")
LANES = 128
PARTS = 1
LIMIT = 20 * 1024 * 1024
HALF = 0.5


def normalize(raw_rows):
    row_norm = jnp.sqrt(jnp.sum(raw_rows * raw_rows, axis=1, keepdims=True) + epsilon)
    return (raw_rows / row_norm, row_norm)


def back_norm(unit_rows, row_norm, gradient):
    return (gradient - unit_rows * jnp.sum(unit_rows * gradient, axis=1, keepdims=True)) / row_norm


def low(rows):
    return rows.astype(jnp.bfloat16).astype(jnp.float32)


def loss_and_sigmoid(values):
    small = jnp.exp(-jnp.abs(values))
    loss = jnp.maximum(values, 0.0) + jnp.log1p(small)
    return loss, jnp.where(values >= 0, 1.0, small) / (1.0 + small)


def own_pairs(image_low, text_low, heat, offset):
    return jnp.sum(image_low * text_low, axis=1, keepdims=True) * heat + offset


def unit_kernel(heat_ref, offset_ref, picture_ref, caption_ref, image_ref, text_ref, loss_ref):
    image_unit, _ = normalize(picture_ref[...])
    text_unit, _ = normalize(caption_ref[...])
    image_low, text_low = image_unit.astype(jnp.bfloat16), text_unit.astype(jnp.bfloat16)
    image_ref[...] = image_low
    text_ref[...] = text_low
    heat = jnp.exp(jnp.full((1, 1), heat_ref[0], jnp.float32))
    logits = own_pairs(image_low.astype(jnp.float32), text_low.astype(jnp.float32), heat, offset_ref[0])
    loss, _ = loss_and_sigmoid(-logits)
    loss_ref[...] = loss


def unit_rows(heat_exponent, offset_added, pictures, captions):
    rows = pictures.shape[0]
    return pl.pallas_call(
        unit_kernel,
        in_specs=[pl.BlockSpec(memory_space=pltpu.SMEM)] * 2 + [pl.BlockSpec(memory_space=pltpu.VMEM)] * 2,
        out_shape=[
            jax.ShapeDtypeStruct(pictures.shape, jnp.bfloat16),
            jax.ShapeDtypeStruct(captions.shape, jnp.bfloat16),
            jax.ShapeDtypeStruct((rows, 1), jnp.float32),
        ],
    )(heat_exponent, offset_added, pictures, captions)


def pieces(total, shape):
    first = low(total)
    second = low(total - first)
    third = total - first - second
    lane = lax.broadcasted_iota(jnp.int32, shape, len(shape) - 1)
    spread = jnp.where(lane == 0, first, jnp.where(lane == 1, second, jnp.where(lane == 2, third, 0.0)))
    return spread.astype(jnp.bfloat16)


def pair_kernel(place_ref, heat_ref, offset_ref, own_loss_ref, near_ref, far_ref, text_ref, weight_ref, text_out_ref):
    rows = own_loss_ref.shape[0]
    half, width = near_ref.shape
    count = text_ref.shape[0] // PARTS
    heat = jnp.exp(jnp.full((1, 1), heat_ref[0], jnp.float32))
    total = jnp.sum(own_loss_ref[...], axis=0, keepdims=True)
    for part in range(PARTS):
        columns = slice(part * count, (part + 1) * count)
        texts = text_ref[columns]
        text_part = None
        for place, image_ref in enumerate((near_ref, far_ref)):
            images = image_ref[...]
            logits = lax.dot_general(
                images, texts, (((1,), (1,)), ((), ())), preferred_element_type=jnp.float32
            )
            logits = logits * heat + offset_ref[0]
            loss, sigmoid = loss_and_sigmoid(logits)
            weights = heat * sigmoid
            if image_ref is near_ref:
                image_row = lax.broadcasted_iota(jnp.int32, logits.shape, 0)
                text_row = lax.broadcasted_iota(jnp.int32, logits.shape, 1) + (part * count - place_ref[0])
                match = (image_row == text_row) & (image_row < rows)
                weights = jnp.where(match, 0.0, weights)
                loss = jnp.where(match, 0.0, loss)
            weights = weights.astype(jnp.bfloat16)
            weight_ref[place * half : (place + 1) * half, columns] = weights
            total += jnp.sum(jnp.sum(loss, axis=0, keepdims=True), axis=1, keepdims=True)
            term = lax.dot_general(
                weights, images, (((0,), (0,)), ((), ())), preferred_element_type=jnp.float32
            )
            text_part = term if text_part is None else text_part + term
        text_out_ref[columns, :width] = text_part.astype(jnp.bfloat16)
    text_out_ref[:, width:] = pieces(total, (text_out_ref.shape[0], LANES))


def pair_terms(place, heat_exponent, offset_added, own_loss, near, far, texts):
    half, width = near.shape
    count = texts.shape[0]
    return pl.pallas_call(
        pair_kernel,
        in_specs=[pl.BlockSpec(memory_space=pltpu.SMEM)] * 3 + [pl.BlockSpec(memory_space=pltpu.VMEM)] * 4,
        out_shape=[
            jax.ShapeDtypeStruct((2 * half, count), jnp.bfloat16),
            jax.ShapeDtypeStruct((count, width + LANES), jnp.bfloat16),
        ],
        compiler_params=pltpu.CompilerParams(vmem_limit_bytes=LIMIT),
        cost_estimate=pl.CostEstimate(
            flops=8 * half * count * width, bytes_accessed=8 * half * width, transcendentals=6 * half * count
        ),
    )(place, heat_exponent, offset_added, own_loss, near, far, texts)


def image_kernel(weight_ref, text_ref, near_ref, far_ref):
    half = near_ref.shape[0]
    texts = text_ref[...]
    far_ref[...] = jnp.dot(weight_ref[half:], texts, preferred_element_type=jnp.float32)
    near_ref[...] = jnp.dot(weight_ref[:half], texts, preferred_element_type=jnp.float32)


def image_terms(weights, texts):
    half, width = weights.shape[0] // 2, texts.shape[1]
    return pl.pallas_call(
        image_kernel,
        in_specs=[pl.BlockSpec(memory_space=pltpu.VMEM)] * 2,
        out_shape=[jax.ShapeDtypeStruct((half, width), jnp.float32)] * 2,
        compiler_params=pltpu.CompilerParams(vmem_limit_bytes=LIMIT),
        cost_estimate=pl.CostEstimate(
            flops=4 * half * texts.shape[0] * width, bytes_accessed=16 * half * width, transcendentals=0
        ),
    )(weights, texts)


def grad_kernel(
    heat_ref, offset_ref, picture_ref, caption_ref, image_sum_ref, text_sum_ref, image_ref, text_ref
):
    image_unit, image_norm = normalize(picture_ref[...])
    text_unit, text_norm = normalize(caption_ref[...])
    image_low, text_low = low(image_unit), low(text_unit)
    heat = jnp.exp(jnp.full((1, 1), heat_ref[0], jnp.float32))
    _, sigmoid = loss_and_sigmoid(-own_pairs(image_low, text_low, heat, offset_ref[0]))
    weights = low(-sigmoid * heat)
    image_ref[...] = back_norm(image_unit, image_norm, image_sum_ref[...] + weights * text_low)
    text_ref[...] = back_norm(text_unit, text_norm, text_sum_ref[...] + weights * image_low)


def gradients(heat_exponent, offset_added, pictures, captions, image_sum, text_sum):
    return pl.pallas_call(
        grad_kernel,
        in_specs=[pl.BlockSpec(memory_space=pltpu.SMEM)] * 2 + [pl.BlockSpec(memory_space=pltpu.VMEM)] * 4,
        out_shape=[jax.ShapeDtypeStruct(pictures.shape, jnp.float32)] * 2,
    )(heat_exponent, offset_added, pictures, captions, image_sum, text_sum)


def swapped(value, axis, step):
    return lax.ppermute(value, axis, [(i, i ^ step) for i in range(lax.axis_size(axis))])


def doubled(value, axis, step):
    return jnp.concatenate([value, swapped(value, axis, step)], axis=0)


def halved(value, axis, step):
    half = value.shape[0] // 2
    sent = (value[half:] * HALF).astype(jnp.float16)
    return value[:half] + swapped(sent, axis, step).astype(jnp.float32) * (1 / HALF)


def shards(picture_vectors, caption_vectors, heat_exponent, offset_added):
    rows, width = picture_vectors.shape
    plane, column = lax.axis_size(PLANE), lax.axis_size(COLUMN)
    steps = [1 << bit for bit in range(lax.axis_size("zl").bit_length() - 1)]
    image_low, text_low, own_loss = unit_rows(heat_exponent, offset_added, picture_vectors, caption_vectors)

    texts = doubled(text_low, "zh", 1)
    texts = lax.all_to_all(jnp.broadcast_to(texts[None], (plane, *texts.shape)), PLANE, 0, 0)
    texts = texts.reshape(plane * 2 * rows, width)
    near = image_low
    for step in reversed(steps):
        near = doubled(near, "zl", step)
    near = doubled(near, "xl", 1)
    near, texts = lax.optimization_barrier((near, texts))
    far = swapped(near, "c", 1)

    place = (lax.axis_index(PLANE) * 2 * rows).astype(jnp.int32).reshape(1)
    weights, text_part = pair_terms(place, heat_exponent, offset_added, own_loss, near, far, texts)
    text_parts = lax.all_to_all(text_part.reshape(plane, 2 * rows, width + LANES), PLANE, 0, 0)

    near_part, far_part = image_terms(weights, texts)
    image_sum = halved(near_part + swapped(far_part, "c", 1), "xl", 1)
    for step in steps:
        image_sum = halved(image_sum, "zl", step)

    plane_loss = jnp.sum(text_parts[:, 0, width : width + 3].astype(jnp.float32))
    losses = lax.all_to_all(jnp.broadcast_to(plane_loss, (column, 1, LANES)), COLUMN, 0, 0)
    loss_mean = (jnp.sum(losses[:, 0, 0]) / (rows * lax.axis_size(AXES))).reshape(1)
    text_sum = jnp.sum(text_parts[:, :, :width].astype(jnp.float32), axis=0)
    text_sum = halved(text_sum, "zh", 1)
    image_grads, text_grads = gradients(
        heat_exponent, offset_added, picture_vectors, caption_vectors, image_sum, text_sum
    )
    return (loss_mean, image_grads, text_grads)


def solution(mesh):
    fine = Mesh(mesh.devices.reshape(SIZES), AXES)
    in_specs = (P(AXES, None), P(AXES, None), P(), P())
    out_specs = (P(), P(AXES, None), P(AXES, None))
    return jax.shard_map(shards, mesh=fine, in_specs=in_specs, out_specs=out_specs, check_vma=False)
```

```python
import jax
import jax.numpy as jnp
from jax import lax
from jax.experimental import pallas as pl
from jax.experimental.pallas import tpu as pltpu
from jax.sharding import Mesh, PartitionSpec as P

epsilon = 1e-06
AXES = ("zl", "x", "c", "y", "zh")
SIZES = (8, 4, 2, 4, 2)
PLANE = ("x", "y")
COLUMN = ("zl", "c", "zh")
LANES = 128
LIMIT = 20 * 1024 * 1024
HALF = 0.5


def normalize(raw_rows):
    row_norm = jnp.sqrt(jnp.sum(raw_rows * raw_rows, axis=1, keepdims=True) + epsilon)
    return (raw_rows / row_norm, row_norm)


def back_norm(unit_rows, row_norm, gradient):
    return (gradient - unit_rows * jnp.sum(unit_rows * gradient, axis=1, keepdims=True)) / row_norm


def low(rows):
    return rows.astype(jnp.bfloat16).astype(jnp.float32)


def loss_and_sigmoid(values):
    small = jnp.exp(-jnp.abs(values))
    loss = jnp.maximum(values, 0.0) + jnp.log1p(small)
    return loss, jnp.where(values >= 0, 1.0, small) / (1.0 + small)


def own_pairs(image_low, text_low, heat, offset):
    return jnp.sum(image_low * text_low, axis=1, keepdims=True) * heat + offset


def unit_kernel(heat_ref, offset_ref, picture_ref, caption_ref, image_ref, own_ref, text_ref, loss_ref):
    image_unit, _ = normalize(picture_ref[...])
    text_unit, _ = normalize(caption_ref[...])
    image_low, text_low = image_unit.astype(jnp.bfloat16), text_unit.astype(jnp.bfloat16)
    image_ref[...] = image_low
    text_ref[...] = jnp.broadcast_to(jnp.concatenate([text_low, text_low], axis=0)[None], text_ref.shape)
    own_ref[...] = text_low
    heat = jnp.exp(jnp.full((1, 1), heat_ref[0], jnp.float32))
    logits = own_pairs(image_low.astype(jnp.float32), text_low.astype(jnp.float32), heat, offset_ref[0])
    loss, _ = loss_and_sigmoid(-logits)
    loss_ref[...] = loss


def unit_rows(copies, heat_exponent, offset_added, pictures, captions):
    rows, width = pictures.shape
    return pl.pallas_call(
        unit_kernel,
        in_specs=[pl.BlockSpec(memory_space=pltpu.SMEM)] * 2 + [pl.BlockSpec(memory_space=pltpu.VMEM)] * 2,
        out_shape=[
            jax.ShapeDtypeStruct(pictures.shape, jnp.bfloat16),
            jax.ShapeDtypeStruct(captions.shape, jnp.bfloat16),
            jax.ShapeDtypeStruct((copies, 2 * rows, width), jnp.bfloat16),
            jax.ShapeDtypeStruct((rows, 1), jnp.float32),
        ],
    )(heat_exponent, offset_added, pictures, captions)


def pieces(total, shape):
    first = low(total)
    second = low(total - first)
    third = total - first - second
    lane = lax.broadcasted_iota(jnp.int32, shape, len(shape) - 1)
    spread = jnp.where(lane == 0, first, jnp.where(lane == 1, second, jnp.where(lane == 2, third, 0.0)))
    return spread.astype(jnp.bfloat16)


def pair_kernel(
    place_ref, heat_ref, offset_ref, own_loss_ref, near_ref, far_ref, text_ref, weight_ref, far_out_ref, loss_ref
):
    rows = own_loss_ref.shape[0]
    texts = text_ref[...]
    heat = jnp.exp(jnp.full((1, 1), heat_ref[0], jnp.float32))
    total = jnp.sum(own_loss_ref[...], axis=0, keepdims=True)
    for place, image_ref in enumerate((near_ref, far_ref)):
        logits = lax.dot_general(
            image_ref[...], texts, (((1,), (1,)), ((), ())), preferred_element_type=jnp.float32
        )
        logits = logits * heat + offset_ref[0]
        loss, sigmoid = loss_and_sigmoid(logits)
        weights = heat * sigmoid
        if image_ref is near_ref:
            image_row = lax.broadcasted_iota(jnp.int32, logits.shape, 0)
            text_row = lax.broadcasted_iota(jnp.int32, logits.shape, 1) - place_ref[0]
            match = (image_row == text_row) & (image_row < rows)
            weights = jnp.where(match, 0.0, weights)
            loss = jnp.where(match, 0.0, loss)
        weights = weights.astype(jnp.bfloat16)
        weight_ref[place] = weights
        total += jnp.sum(jnp.sum(loss, axis=0, keepdims=True), axis=1, keepdims=True)
    far_out_ref[...] = jnp.dot(weights, texts, preferred_element_type=jnp.float32)
    loss_ref[...] = jnp.broadcast_to(total, loss_ref.shape)


def pair_weights(place, heat_exponent, offset_added, own_loss, near, far, texts):
    half, width = near.shape
    count = texts.shape[0]
    return pl.pallas_call(
        pair_kernel,
        in_specs=[pl.BlockSpec(memory_space=pltpu.SMEM)] * 3 + [pl.BlockSpec(memory_space=pltpu.VMEM)] * 4,
        out_shape=[
            jax.ShapeDtypeStruct((2, half, count), jnp.bfloat16),
            jax.ShapeDtypeStruct((half, width), jnp.float32),
            jax.ShapeDtypeStruct((8, LANES), jnp.float32),
        ],
        compiler_params=pltpu.CompilerParams(vmem_limit_bytes=LIMIT),
        cost_estimate=pl.CostEstimate(
            flops=6 * half * count * width, bytes_accessed=8 * half * width, transcendentals=6 * half * count
        ),
    )(place, heat_exponent, offset_added, own_loss, near, far, texts)


def terms_kernel(weight_ref, loss_ref, near_ref, far_ref, text_ref, near_out_ref, text_out_ref):
    width = near_ref.shape[1]
    text_part = lax.dot_general(
        weight_ref[0], near_ref[...], (((0,), (0,)), ((), ())), preferred_element_type=jnp.float32
    )
    text_part += lax.dot_general(
        weight_ref[1], far_ref[...], (((0,), (0,)), ((), ())), preferred_element_type=jnp.float32
    )
    text_out_ref[:, :width] = text_part.astype(jnp.bfloat16)
    text_out_ref[:, width:] = pieces(loss_ref[:1, :1], (text_out_ref.shape[0], LANES))
    near_out_ref[...] = jnp.dot(weight_ref[0], text_ref[...], preferred_element_type=jnp.float32)


def pair_terms(weights, loss, near, far, texts):
    count, width = texts.shape
    return pl.pallas_call(
        terms_kernel,
        in_specs=[pl.BlockSpec(memory_space=pltpu.VMEM)] * 5,
        out_shape=[
            jax.ShapeDtypeStruct(near.shape, jnp.float32),
            jax.ShapeDtypeStruct((count, width + LANES), jnp.bfloat16),
        ],
        compiler_params=pltpu.CompilerParams(vmem_limit_bytes=LIMIT),
        cost_estimate=pl.CostEstimate(flops=3 * weights.size * width, bytes_accessed=16 * near.size, transcendentals=0),
    )(weights, loss, near, far, texts)


def grad_kernel(
    heat_ref, offset_ref, picture_ref, caption_ref, image_sum_ref, text_sum_ref, image_ref, text_ref
):
    image_unit, image_norm = normalize(picture_ref[...])
    text_unit, text_norm = normalize(caption_ref[...])
    image_low, text_low = low(image_unit), low(text_unit)
    heat = jnp.exp(jnp.full((1, 1), heat_ref[0], jnp.float32))
    _, sigmoid = loss_and_sigmoid(-own_pairs(image_low, text_low, heat, offset_ref[0]))
    weights = low(-sigmoid * heat)
    image_ref[...] = back_norm(image_unit, image_norm, image_sum_ref[...] + weights * text_low)
    text_ref[...] = back_norm(text_unit, text_norm, text_sum_ref[...] + weights * image_low)


def gradients(heat_exponent, offset_added, pictures, captions, image_sum, text_sum):
    return pl.pallas_call(
        grad_kernel,
        in_specs=[pl.BlockSpec(memory_space=pltpu.SMEM)] * 2 + [pl.BlockSpec(memory_space=pltpu.VMEM)] * 4,
        out_shape=[jax.ShapeDtypeStruct(pictures.shape, jnp.float32)] * 2,
    )(heat_exponent, offset_added, pictures, captions, image_sum, text_sum)


def swapped(value, axis, step):
    return lax.ppermute(value, axis, [(i, i ^ step) for i in range(lax.axis_size(axis))])


def doubled(value, axis, step):
    return jnp.concatenate([value, swapped(value, axis, step)], axis=0)


def halved(value, axis, step):
    half = value.shape[0] // 2
    sent = (value[half:] * HALF).astype(jnp.float16)
    return value[:half] + swapped(sent, axis, step).astype(jnp.float32) * (1 / HALF)


def shards(picture_vectors, caption_vectors, heat_exponent, offset_added):
    rows, width = picture_vectors.shape
    plane, column = lax.axis_size(PLANE), lax.axis_size(COLUMN)
    steps = [1 << bit for bit in range(lax.axis_size("zl").bit_length() - 1)]
    image_low, text_low, copies, own_loss = unit_rows(
        plane, heat_exponent, offset_added, picture_vectors, caption_vectors
    )

    other_low = jnp.broadcast_to(swapped(text_low, "zh", 1)[None], (plane, rows, width))
    texts = lax.all_to_all(lax.dynamic_update_slice(copies, other_low, (0, rows, 0)), PLANE, 0, 0)
    texts = texts.reshape(plane * 2 * rows, width)
    near = image_low
    for step in reversed(steps):
        near = doubled(near, "zl", step)
    far = swapped(near, "c", 1)

    place = (lax.axis_index(PLANE) * 2 * rows).astype(jnp.int32).reshape(1)
    weights, far_part, loss = pair_weights(place, heat_exponent, offset_added, own_loss, near, far, texts)
    far_part = swapped(far_part, "c", 1)
    near_part, text_part = pair_terms(weights, loss, near, far, texts)
    text_parts = lax.all_to_all(text_part.reshape(plane, 2 * rows, width + LANES), PLANE, 0, 0)
    image_sum = near_part + far_part
    for step in steps:
        image_sum = halved(image_sum, "zl", step)

    plane_loss = jnp.sum(text_parts[:, 0, width : width + 3].astype(jnp.float32))
    losses = lax.all_to_all(jnp.broadcast_to(plane_loss, (column, 1, LANES)), COLUMN, 0, 0)
    loss_mean = (jnp.sum(losses[:, 0, 0]) / (rows * lax.axis_size(AXES))).reshape(1)
    text_sum = jnp.sum(text_parts[:, :, :width].astype(jnp.float32), axis=0)
    text_sum = halved(text_sum, "zh", 1)
    image_grads, text_grads = gradients(
        heat_exponent, offset_added, picture_vectors, caption_vectors, image_sum, text_sum
    )
    return (loss_mean, image_grads, text_grads)


def solution(mesh):
    fine = Mesh(mesh.devices.reshape(SIZES), AXES)
    in_specs = (P(AXES, None), P(AXES, None), P(), P())
    out_specs = (P(), P(AXES, None), P(AXES, None))
    return jax.shard_map(shards, mesh=fine, in_specs=in_specs, out_specs=out_specs, check_vma=False)
```

```python
import jax
import jax.numpy as jnp
from jax import lax
from jax.experimental import pallas as pl
from jax.experimental.pallas import tpu as pltpu
from jax.sharding import Mesh, PartitionSpec as P

epsilon = 1e-06
AXES = ("zl", "x", "c", "y", "zh")
SIZES = (8, 4, 2, 4, 2)
PLANE = ("x", "y")
COLUMN = ("zl", "c", "zh")
LANES = 128
LIMIT = 20 * 1024 * 1024
HALF = 0.5


def normalize(raw_rows):
    row_norm = jnp.sqrt(jnp.sum(raw_rows * raw_rows, axis=1, keepdims=True) + epsilon)
    return (raw_rows / row_norm, row_norm)


def back_norm(unit_rows, row_norm, gradient):
    return (gradient - unit_rows * jnp.sum(unit_rows * gradient, axis=1, keepdims=True)) / row_norm


def low(rows):
    return rows.astype(jnp.bfloat16).astype(jnp.float32)


def loss_and_sigmoid(values):
    small = jnp.exp(-jnp.abs(values))
    loss = jnp.maximum(values, 0.0) + jnp.log1p(small)
    return loss, jnp.where(values >= 0, 1.0, small) / (1.0 + small)


def own_pairs(image_low, text_low, heat, offset):
    return jnp.sum(image_low * text_low, axis=1, keepdims=True) * heat + offset


def unit_kernel(heat_ref, offset_ref, picture_ref, caption_ref, image_ref, own_ref, text_ref, loss_ref):
    image_unit, _ = normalize(picture_ref[...])
    text_unit, _ = normalize(caption_ref[...])
    image_low, text_low = image_unit.astype(jnp.bfloat16), text_unit.astype(jnp.bfloat16)
    image_ref[...] = image_low
    text_ref[...] = jnp.broadcast_to(jnp.concatenate([text_low, text_low], axis=0)[None], text_ref.shape)
    own_ref[...] = text_low
    heat = jnp.exp(jnp.full((1, 1), heat_ref[0], jnp.float32))
    logits = own_pairs(image_low.astype(jnp.float32), text_low.astype(jnp.float32), heat, offset_ref[0])
    loss, _ = loss_and_sigmoid(-logits)
    loss_ref[...] = loss


def unit_rows(copies, heat_exponent, offset_added, pictures, captions):
    rows, width = pictures.shape
    return pl.pallas_call(
        unit_kernel,
        in_specs=[pl.BlockSpec(memory_space=pltpu.SMEM)] * 2 + [pl.BlockSpec(memory_space=pltpu.VMEM)] * 2,
        out_shape=[
            jax.ShapeDtypeStruct(pictures.shape, jnp.bfloat16),
            jax.ShapeDtypeStruct(captions.shape, jnp.bfloat16),
            jax.ShapeDtypeStruct((copies, 2 * rows, width), jnp.bfloat16),
            jax.ShapeDtypeStruct((rows, 1), jnp.float32),
        ],
    )(heat_exponent, offset_added, pictures, captions)


def pieces(total, shape):
    first = low(total)
    second = low(total - first)
    third = total - first - second
    lane = lax.broadcasted_iota(jnp.int32, shape, len(shape) - 1)
    spread = jnp.where(lane == 0, first, jnp.where(lane == 1, second, jnp.where(lane == 2, third, 0.0)))
    return spread.astype(jnp.bfloat16)


def pair_kernel(
    place_ref, heat_ref, offset_ref, own_loss_ref, near_ref, far_ref, text_ref, weight_ref, far_out_ref, loss_ref
):
    rows = own_loss_ref.shape[0]
    texts = text_ref[...]
    heat = jnp.exp(jnp.full((1, 1), heat_ref[0], jnp.float32))
    total = jnp.sum(own_loss_ref[...], axis=0, keepdims=True)
    for place, image_ref in enumerate((near_ref, far_ref)):
        logits = lax.dot_general(
            image_ref[...], texts, (((1,), (1,)), ((), ())), preferred_element_type=jnp.float32
        )
        logits = logits * heat + offset_ref[0]
        loss, sigmoid = loss_and_sigmoid(logits)
        weights = heat * sigmoid
        if image_ref is near_ref:
            image_row = lax.broadcasted_iota(jnp.int32, logits.shape, 0)
            text_row = lax.broadcasted_iota(jnp.int32, logits.shape, 1) - place_ref[0]
            match = (image_row == text_row) & (image_row < rows)
            weights = jnp.where(match, 0.0, weights)
            loss = jnp.where(match, 0.0, loss)
        weights = weights.astype(jnp.bfloat16)
        weight_ref[place] = weights
        total += jnp.sum(jnp.sum(loss, axis=0, keepdims=True), axis=1, keepdims=True)
    far_out_ref[...] = jnp.dot(weights, texts, preferred_element_type=jnp.float32)
    loss_ref[...] = jnp.broadcast_to(total, loss_ref.shape)


def pair_weights(place, heat_exponent, offset_added, own_loss, near, far, texts):
    half, width = near.shape
    count = texts.shape[0]
    return pl.pallas_call(
        pair_kernel,
        in_specs=[pl.BlockSpec(memory_space=pltpu.SMEM)] * 3 + [pl.BlockSpec(memory_space=pltpu.VMEM)] * 4,
        out_shape=[
            jax.ShapeDtypeStruct((2, half, count), jnp.bfloat16),
            jax.ShapeDtypeStruct((half, width), jnp.float32),
            jax.ShapeDtypeStruct((8, LANES), jnp.float32),
        ],
        compiler_params=pltpu.CompilerParams(vmem_limit_bytes=LIMIT),
        cost_estimate=pl.CostEstimate(
            flops=6 * half * count * width, bytes_accessed=8 * half * width, transcendentals=6 * half * count
        ),
    )(place, heat_exponent, offset_added, own_loss, near, far, texts)


def terms_kernel(weight_ref, loss_ref, near_ref, far_ref, text_ref, near_out_ref, text_out_ref):
    width = near_ref.shape[1]
    text_part = lax.dot_general(
        weight_ref[0], near_ref[...], (((0,), (0,)), ((), ())), preferred_element_type=jnp.float32
    )
    text_part += lax.dot_general(
        weight_ref[1], far_ref[...], (((0,), (0,)), ((), ())), preferred_element_type=jnp.float32
    )
    text_out_ref[:, :width] = text_part.astype(jnp.bfloat16)
    text_out_ref[:, width:] = pieces(loss_ref[:1, :1], (text_out_ref.shape[0], LANES))
    near_out_ref[...] = jnp.dot(weight_ref[0], text_ref[...], preferred_element_type=jnp.float32)


def pair_terms(weights, loss, near, far, texts):
    count, width = texts.shape
    return pl.pallas_call(
        terms_kernel,
        in_specs=[pl.BlockSpec(memory_space=pltpu.VMEM)] * 5,
        out_shape=[
            jax.ShapeDtypeStruct(near.shape, jnp.float32),
            jax.ShapeDtypeStruct((count, width + LANES), jnp.bfloat16),
        ],
        compiler_params=pltpu.CompilerParams(vmem_limit_bytes=LIMIT),
        cost_estimate=pl.CostEstimate(flops=3 * weights.size * width, bytes_accessed=16 * near.size, transcendentals=0),
    )(weights, loss, near, far, texts)


def grad_kernel(heat_ref, offset_ref, row_ref, low_ref, partner_ref, sum_ref, grad_ref):
    unit, norm = normalize(row_ref[...])
    partner_low = partner_ref[...].astype(jnp.float32)
    heat = jnp.exp(jnp.full((1, 1), heat_ref[0], jnp.float32))
    logits = own_pairs(low_ref[...].astype(jnp.float32), partner_low, heat, offset_ref[0])
    _, sigmoid = loss_and_sigmoid(-logits)
    grad_ref[...] = back_norm(unit, norm, sum_ref[...] + low(-sigmoid * heat) * partner_low)


def gradients(heat_exponent, offset_added, vectors, lows, partners, sums):
    return pl.pallas_call(
        grad_kernel,
        in_specs=[pl.BlockSpec(memory_space=pltpu.SMEM)] * 2 + [pl.BlockSpec(memory_space=pltpu.VMEM)] * 4,
        out_shape=jax.ShapeDtypeStruct(vectors.shape, jnp.float32),
    )(heat_exponent, offset_added, vectors, lows, partners, sums)


def swapped(value, axis, step):
    return lax.ppermute(value, axis, [(i, i ^ step) for i in range(lax.axis_size(axis))])


def doubled(value, axis, step):
    return jnp.concatenate([value, swapped(value, axis, step)], axis=0)


def halved(value, axis, step):
    half = value.shape[0] // 2
    sent = (value[half:] * HALF).astype(jnp.float16)
    return value[:half] + swapped(sent, axis, step).astype(jnp.float32) * (1 / HALF)


def shards(picture_vectors, caption_vectors, heat_exponent, offset_added):
    rows, width = picture_vectors.shape
    plane, column = lax.axis_size(PLANE), lax.axis_size(COLUMN)
    steps = [1 << bit for bit in range(lax.axis_size("zl").bit_length() - 1)]
    image_low, text_low, copies, own_loss = unit_rows(
        plane, heat_exponent, offset_added, picture_vectors, caption_vectors
    )

    other_low = jnp.broadcast_to(swapped(text_low, "zh", 1)[None], (plane, rows, width))
    texts = lax.all_to_all(lax.dynamic_update_slice(copies, other_low, (0, rows, 0)), PLANE, 0, 0)
    texts = texts.reshape(plane * 2 * rows, width)
    near = image_low
    for step in reversed(steps):
        near = doubled(near, "zl", step)
    far = swapped(near, "c", 1)

    place = (lax.axis_index(PLANE) * 2 * rows).astype(jnp.int32).reshape(1)
    weights, far_part, loss = pair_weights(place, heat_exponent, offset_added, own_loss, near, far, texts)
    far_part = swapped(far_part, "c", 1)
    near_part, text_part = pair_terms(weights, loss, near, far, texts)
    text_parts = lax.all_to_all(text_part.reshape(plane, 2 * rows, width + LANES), PLANE, 0, 0)
    image_sum = near_part + far_part
    for step in steps:
        image_sum = halved(image_sum, "zl", step)

    plane_loss = jnp.sum(text_parts[:, 0, width : width + 3].astype(jnp.float32))
    losses = lax.all_to_all(jnp.broadcast_to(plane_loss, (column, 1, LANES)), COLUMN, 0, 0)
    loss_mean = (jnp.sum(losses[:, 0, 0]) / (rows * lax.axis_size(AXES))).reshape(1)
    text_sum = jnp.sum(text_parts[:, :, :width].astype(jnp.float32), axis=0)
    arrived = swapped((text_sum[rows:] * HALF).astype(jnp.float16), "zh", 1)
    arrived, loss_mean = lax.optimization_barrier((arrived, loss_mean))
    text_sum = text_sum[:rows] + arrived.astype(jnp.float32) * (1 / HALF)
    image_grads = gradients(heat_exponent, offset_added, picture_vectors, image_low, text_low, image_sum)
    text_grads = gradients(heat_exponent, offset_added, caption_vectors, text_low, image_low, text_sum)
    return (loss_mean, image_grads, text_grads)


def solution(mesh):
    fine = Mesh(mesh.devices.reshape(SIZES), AXES)
    in_specs = (P(AXES, None), P(AXES, None), P(), P())
    out_specs = (P(), P(AXES, None), P(AXES, None))
    return jax.shard_map(shards, mesh=fine, in_specs=in_specs, out_specs=out_specs, check_vma=False)
```

```python
import jax
import jax.numpy as jnp
from jax import lax
from jax.experimental import pallas as pl
from jax.experimental.pallas import tpu as pltpu
from jax.sharding import Mesh, PartitionSpec as P

epsilon = 1e-06
AXES = ("zm", "zl", "x", "c", "y", "zh")
SIZES = (2, 4, 4, 2, 4, 2)
PLANE = ("x", "y")
COLUMN = ("zm", "zl", "c", "zh")
LANES = 128
LIMIT = 20 * 1024 * 1024
HALF = 0.5


def normalize(raw_rows):
    row_norm = jnp.sqrt(jnp.sum(raw_rows * raw_rows, axis=1, keepdims=True) + epsilon)
    return (raw_rows / row_norm, row_norm)


def back_norm(unit_rows, row_norm, gradient):
    return (gradient - unit_rows * jnp.sum(unit_rows * gradient, axis=1, keepdims=True)) / row_norm


def low(rows):
    return rows.astype(jnp.bfloat16).astype(jnp.float32)


def loss_and_sigmoid(values):
    small = jnp.exp(-jnp.abs(values))
    loss = jnp.maximum(values, 0.0) + jnp.log1p(small)
    return loss, jnp.where(values >= 0, 1.0, small) / (1.0 + small)


def own_pairs(image_low, text_low, heat, offset):
    return jnp.sum(image_low * text_low, axis=1, keepdims=True) * heat + offset


def unit_kernel(heat_ref, offset_ref, picture_ref, caption_ref, image_ref, own_ref, text_ref, loss_ref):
    image_unit, _ = normalize(picture_ref[...])
    text_unit, _ = normalize(caption_ref[...])
    image_low, text_low = image_unit.astype(jnp.bfloat16), text_unit.astype(jnp.bfloat16)
    image_ref[...] = image_low
    text_ref[...] = jnp.broadcast_to(jnp.concatenate([text_low, text_low], axis=0)[None], text_ref.shape)
    own_ref[...] = text_low
    heat = jnp.exp(jnp.full((1, 1), heat_ref[0], jnp.float32))
    logits = own_pairs(image_low.astype(jnp.float32), text_low.astype(jnp.float32), heat, offset_ref[0])
    loss, _ = loss_and_sigmoid(-logits)
    loss_ref[...] = loss


def unit_rows(copies, heat_exponent, offset_added, pictures, captions):
    rows, width = pictures.shape
    return pl.pallas_call(
        unit_kernel,
        in_specs=[pl.BlockSpec(memory_space=pltpu.SMEM)] * 2 + [pl.BlockSpec(memory_space=pltpu.VMEM)] * 2,
        out_shape=[
            jax.ShapeDtypeStruct(pictures.shape, jnp.bfloat16),
            jax.ShapeDtypeStruct(captions.shape, jnp.bfloat16),
            jax.ShapeDtypeStruct((copies, 2 * rows, width), jnp.bfloat16),
            jax.ShapeDtypeStruct((rows, 1), jnp.float32),
        ],
    )(heat_exponent, offset_added, pictures, captions)


def pieces(total, shape):
    first = low(total)
    second = low(total - first)
    third = total - first - second
    lane = lax.broadcasted_iota(jnp.int32, shape, len(shape) - 1)
    spread = jnp.where(lane == 0, first, jnp.where(lane == 1, second, jnp.where(lane == 2, third, 0.0)))
    return spread.astype(jnp.bfloat16)


def pair_kernel(
    place_ref, heat_ref, offset_ref, own_loss_ref, near_ref, far_ref, text_ref, weight_ref, far_out_ref, loss_ref
):
    rows = own_loss_ref.shape[0]
    texts = text_ref[...]
    heat = jnp.exp(jnp.full((1, 1), heat_ref[0], jnp.float32))
    total = jnp.sum(own_loss_ref[...], axis=0, keepdims=True)
    for place, image_ref in enumerate((near_ref, far_ref)):
        logits = lax.dot_general(
            image_ref[...], texts, (((1,), (1,)), ((), ())), preferred_element_type=jnp.float32
        )
        logits = logits * heat + offset_ref[0]
        loss, sigmoid = loss_and_sigmoid(logits)
        weights = heat * sigmoid
        if image_ref is near_ref:
            image_row = lax.broadcasted_iota(jnp.int32, logits.shape, 0)
            text_row = lax.broadcasted_iota(jnp.int32, logits.shape, 1) - place_ref[0]
            match = (image_row == text_row) & (image_row < rows)
            weights = jnp.where(match, 0.0, weights)
            loss = jnp.where(match, 0.0, loss)
        weights = weights.astype(jnp.bfloat16)
        weight_ref[place] = weights
        total += jnp.sum(jnp.sum(loss, axis=0, keepdims=True), axis=1, keepdims=True)
    far_out_ref[...] = jnp.dot(weights, texts, preferred_element_type=jnp.float32)
    loss_ref[...] = jnp.broadcast_to(total, loss_ref.shape)


def pair_weights(place, heat_exponent, offset_added, own_loss, near, far, texts):
    half, width = near.shape
    count = texts.shape[0]
    return pl.pallas_call(
        pair_kernel,
        in_specs=[pl.BlockSpec(memory_space=pltpu.SMEM)] * 3 + [pl.BlockSpec(memory_space=pltpu.VMEM)] * 4,
        out_shape=[
            jax.ShapeDtypeStruct((2, half, count), jnp.bfloat16),
            jax.ShapeDtypeStruct((half, width), jnp.float32),
            jax.ShapeDtypeStruct((8, LANES), jnp.float32),
        ],
        compiler_params=pltpu.CompilerParams(vmem_limit_bytes=LIMIT),
        cost_estimate=pl.CostEstimate(
            flops=6 * half * count * width, bytes_accessed=8 * half * width, transcendentals=6 * half * count
        ),
    )(place, heat_exponent, offset_added, own_loss, near, far, texts)


def terms_kernel(weight_ref, loss_ref, near_ref, far_ref, text_ref, near_out_ref, text_out_ref):
    width = near_ref.shape[1]
    text_part = lax.dot_general(
        weight_ref[0], near_ref[...], (((0,), (0,)), ((), ())), preferred_element_type=jnp.float32
    )
    text_part += lax.dot_general(
        weight_ref[1], far_ref[...], (((0,), (0,)), ((), ())), preferred_element_type=jnp.float32
    )
    text_out_ref[:, :width] = text_part.astype(jnp.bfloat16)
    text_out_ref[:, width:] = pieces(loss_ref[:1, :1], (text_out_ref.shape[0], LANES))
    near_out_ref[...] = jnp.dot(weight_ref[0], text_ref[...], preferred_element_type=jnp.float32)


def pair_terms(weights, loss, near, far, texts):
    count, width = texts.shape
    return pl.pallas_call(
        terms_kernel,
        in_specs=[pl.BlockSpec(memory_space=pltpu.VMEM)] * 5,
        out_shape=[
            jax.ShapeDtypeStruct(near.shape, jnp.float32),
            jax.ShapeDtypeStruct((count, width + LANES), jnp.bfloat16),
        ],
        compiler_params=pltpu.CompilerParams(vmem_limit_bytes=LIMIT),
        cost_estimate=pl.CostEstimate(flops=3 * weights.size * width, bytes_accessed=16 * near.size, transcendentals=0),
    )(weights, loss, near, far, texts)


def grad_kernel(heat_ref, offset_ref, row_ref, low_ref, partner_ref, sum_ref, grad_ref):
    unit, norm = normalize(row_ref[...])
    partner_low = partner_ref[...].astype(jnp.float32)
    heat = jnp.exp(jnp.full((1, 1), heat_ref[0], jnp.float32))
    logits = own_pairs(low_ref[...].astype(jnp.float32), partner_low, heat, offset_ref[0])
    _, sigmoid = loss_and_sigmoid(-logits)
    grad_ref[...] = back_norm(unit, norm, sum_ref[...] + low(-sigmoid * heat) * partner_low)


def gradients(heat_exponent, offset_added, vectors, lows, partners, sums):
    return pl.pallas_call(
        grad_kernel,
        in_specs=[pl.BlockSpec(memory_space=pltpu.SMEM)] * 2 + [pl.BlockSpec(memory_space=pltpu.VMEM)] * 4,
        out_shape=jax.ShapeDtypeStruct(vectors.shape, jnp.float32),
    )(heat_exponent, offset_added, vectors, lows, partners, sums)


def swapped(value, axis, step):
    return lax.ppermute(value, axis, [(i, i ^ step) for i in range(lax.axis_size(axis))])


def doubled(value, axis, step):
    return jnp.concatenate([value, swapped(value, axis, step)], axis=0)


def halved(value, axis, step):
    half = value.shape[0] // 2
    sent = (value[half:] * HALF).astype(jnp.float16)
    return value[:half] + swapped(sent, axis, step).astype(jnp.float32) * (1 / HALF)


def shards(picture_vectors, caption_vectors, heat_exponent, offset_added):
    rows, width = picture_vectors.shape
    plane, column = lax.axis_size(PLANE), lax.axis_size(COLUMN)
    steps = [1 << bit for bit in range(lax.axis_size("zl").bit_length() - 1)]
    image_low, text_low, copies, own_loss = unit_rows(
        plane, heat_exponent, offset_added, picture_vectors, caption_vectors
    )

    other_low = jnp.broadcast_to(swapped(text_low, "zm", 1)[None], (plane, rows, width))
    texts = lax.all_to_all(lax.dynamic_update_slice(copies, other_low, (0, rows, 0)), PLANE, 0, 0)
    texts = texts.reshape(plane * 2 * rows, width)
    near = doubled(image_low, "zh", 1)
    for step in reversed(steps):
        near = doubled(near, "zl", step)
    far = swapped(near, "c", 1)

    place = (lax.axis_index(PLANE) * 2 * rows).astype(jnp.int32).reshape(1)
    weights, far_part, loss = pair_weights(place, heat_exponent, offset_added, own_loss, near, far, texts)
    far_part = swapped(far_part, "c", 1)
    near_part, text_part = pair_terms(weights, loss, near, far, texts)
    text_parts = lax.all_to_all(text_part.reshape(plane, 2 * rows, width + LANES), PLANE, 0, 0)
    image_sum = near_part + far_part
    for step in steps:
        image_sum = halved(image_sum, "zl", step)
    image_sum = halved(image_sum, "zh", 1)

    plane_loss = jnp.sum(text_parts[:, 0, width : width + 3].astype(jnp.float32))
    losses = lax.all_to_all(jnp.broadcast_to(plane_loss, (column, 1, LANES)), COLUMN, 0, 0)
    loss_mean = (jnp.sum(losses[:, 0, 0]) / (rows * lax.axis_size(AXES))).reshape(1)
    text_sum = jnp.sum(text_parts[:, :, :width].astype(jnp.float32), axis=0)
    arrived = swapped((text_sum[rows:] * HALF).astype(jnp.float16), "zm", 1)
    arrived, loss_mean = lax.optimization_barrier((arrived, loss_mean))
    text_sum = text_sum[:rows] + arrived.astype(jnp.float32) * (1 / HALF)
    image_grads = gradients(heat_exponent, offset_added, picture_vectors, image_low, text_low, image_sum)
    text_grads = gradients(heat_exponent, offset_added, caption_vectors, text_low, image_low, text_sum)
    return (loss_mean, image_grads, text_grads)


def solution(mesh):
    fine = Mesh(mesh.devices.reshape(SIZES), AXES)
    in_specs = (P(AXES, None), P(AXES, None), P(), P())
    out_specs = (P(), P(AXES, None), P(AXES, None))
    return jax.shard_map(shards, mesh=fine, in_specs=in_specs, out_specs=out_specs, check_vma=False)
```

```python
import jax
import jax.numpy as jnp
from jax import lax
from jax.experimental import pallas as pl
from jax.experimental.pallas import tpu as pltpu
from jax.sharding import Mesh, PartitionSpec as P

epsilon = 1e-06
AXES = ("zm", "zl", "x", "c", "y", "zh")
SIZES = (2, 4, 4, 2, 4, 2)
PLANE = ("x", "y")
COLUMN = ("zm", "zl", "c", "zh")
LANES = 128
LIMIT = 20 * 1024 * 1024
HALF = 0.5


def normalize(raw_rows):
    row_norm = jnp.sqrt(jnp.sum(raw_rows * raw_rows, axis=1, keepdims=True) + epsilon)
    return (raw_rows / row_norm, row_norm)


def back_norm(unit_rows, row_norm, gradient):
    return (gradient - unit_rows * jnp.sum(unit_rows * gradient, axis=1, keepdims=True)) / row_norm


def low(rows):
    return rows.astype(jnp.bfloat16).astype(jnp.float32)


def loss_and_sigmoid(values):
    small = jnp.exp(-jnp.abs(values))
    loss = jnp.maximum(values, 0.0) + jnp.log1p(small)
    return loss, jnp.where(values >= 0, 1.0, small) / (1.0 + small)


def own_pairs(image_low, text_low, heat, offset):
    return jnp.sum(image_low * text_low, axis=1, keepdims=True) * heat + offset


def unit_kernel(heat_ref, offset_ref, picture_ref, caption_ref, image_ref, own_ref, text_ref, loss_ref):
    image_unit, _ = normalize(picture_ref[...])
    text_unit, _ = normalize(caption_ref[...])
    image_low, text_low = image_unit.astype(jnp.bfloat16), text_unit.astype(jnp.bfloat16)
    image_ref[...] = image_low
    text_ref[...] = jnp.broadcast_to(jnp.concatenate([text_low, text_low], axis=0)[None], text_ref.shape)
    own_ref[...] = text_low
    heat = jnp.exp(jnp.full((1, 1), heat_ref[0], jnp.float32))
    logits = own_pairs(image_low.astype(jnp.float32), text_low.astype(jnp.float32), heat, offset_ref[0])
    loss, _ = loss_and_sigmoid(-logits)
    loss_ref[...] = loss


def unit_rows(copies, heat_exponent, offset_added, pictures, captions):
    rows, width = pictures.shape
    return pl.pallas_call(
        unit_kernel,
        in_specs=[pl.BlockSpec(memory_space=pltpu.SMEM)] * 2 + [pl.BlockSpec(memory_space=pltpu.VMEM)] * 2,
        out_shape=[
            jax.ShapeDtypeStruct(pictures.shape, jnp.bfloat16),
            jax.ShapeDtypeStruct(captions.shape, jnp.bfloat16),
            jax.ShapeDtypeStruct((copies, 2 * rows, width), jnp.bfloat16),
            jax.ShapeDtypeStruct((rows, 1), jnp.float32),
        ],
    )(heat_exponent, offset_added, pictures, captions)


def pieces(total, shape):
    first = low(total)
    second = low(total - first)
    third = total - first - second
    lane = lax.broadcasted_iota(jnp.int32, shape, len(shape) - 1)
    spread = jnp.where(lane == 0, first, jnp.where(lane == 1, second, jnp.where(lane == 2, third, 0.0)))
    return spread.astype(jnp.bfloat16)


def pair_kernel(
    place_ref, heat_ref, offset_ref, own_loss_ref, near_ref, far_ref, text_ref, weight_ref, far_out_ref, loss_ref
):
    rows = own_loss_ref.shape[0]
    texts = text_ref[...]
    heat = jnp.exp(jnp.full((1, 1), heat_ref[0], jnp.float32))
    total = jnp.sum(own_loss_ref[...], axis=0, keepdims=True)
    for place, image_ref in enumerate((near_ref, far_ref)):
        logits = lax.dot_general(
            image_ref[...], texts, (((1,), (1,)), ((), ())), preferred_element_type=jnp.float32
        )
        logits = logits * heat + offset_ref[0]
        loss, sigmoid = loss_and_sigmoid(logits)
        weights = heat * sigmoid
        if image_ref is near_ref:
            image_row = lax.broadcasted_iota(jnp.int32, logits.shape, 0)
            text_row = lax.broadcasted_iota(jnp.int32, logits.shape, 1) - place_ref[0]
            match = (image_row == text_row) & (image_row < rows)
            weights = jnp.where(match, 0.0, weights)
            loss = jnp.where(match, 0.0, loss)
        weights = weights.astype(jnp.bfloat16)
        weight_ref[place] = weights
        total += jnp.sum(jnp.sum(loss, axis=0, keepdims=True), axis=1, keepdims=True)
    far_out_ref[...] = jnp.dot(weights, texts, preferred_element_type=jnp.float32)
    loss_ref[...] = jnp.broadcast_to(total, loss_ref.shape)


def pair_weights(place, heat_exponent, offset_added, own_loss, near, far, texts):
    half, width = near.shape
    count = texts.shape[0]
    return pl.pallas_call(
        pair_kernel,
        in_specs=[pl.BlockSpec(memory_space=pltpu.SMEM)] * 3 + [pl.BlockSpec(memory_space=pltpu.VMEM)] * 4,
        out_shape=[
            jax.ShapeDtypeStruct((2, half, count), jnp.bfloat16),
            jax.ShapeDtypeStruct((half, width), jnp.float32),
            jax.ShapeDtypeStruct((8, LANES), jnp.float32),
        ],
        compiler_params=pltpu.CompilerParams(vmem_limit_bytes=LIMIT),
        cost_estimate=pl.CostEstimate(
            flops=6 * half * count * width, bytes_accessed=8 * half * width, transcendentals=6 * half * count
        ),
    )(place, heat_exponent, offset_added, own_loss, near, far, texts)


def terms_kernel(weight_ref, loss_ref, near_ref, far_ref, text_ref, near_out_ref, text_out_ref):
    width = near_ref.shape[1]
    text_part = lax.dot_general(
        weight_ref[0], near_ref[...], (((0,), (0,)), ((), ())), preferred_element_type=jnp.float32
    )
    text_part += lax.dot_general(
        weight_ref[1], far_ref[...], (((0,), (0,)), ((), ())), preferred_element_type=jnp.float32
    )
    text_out_ref[:, :width] = text_part.astype(jnp.bfloat16)
    text_out_ref[:, width:] = pieces(loss_ref[:1, :1], (text_out_ref.shape[0], LANES))
    near_out_ref[...] = jnp.dot(weight_ref[0], text_ref[...], preferred_element_type=jnp.float32)


def pair_terms(weights, loss, near, far, texts):
    count, width = texts.shape
    return pl.pallas_call(
        terms_kernel,
        in_specs=[pl.BlockSpec(memory_space=pltpu.VMEM)] * 5,
        out_shape=[
            jax.ShapeDtypeStruct(near.shape, jnp.float32),
            jax.ShapeDtypeStruct((count, width + LANES), jnp.bfloat16),
        ],
        compiler_params=pltpu.CompilerParams(vmem_limit_bytes=LIMIT),
        cost_estimate=pl.CostEstimate(flops=3 * weights.size * width, bytes_accessed=16 * near.size, transcendentals=0),
    )(weights, loss, near, far, texts)


def grad_kernel(heat_ref, offset_ref, row_ref, low_ref, partner_ref, sum_ref, grad_ref):
    unit, norm = normalize(row_ref[...])
    partner_low = partner_ref[...].astype(jnp.float32)
    heat = jnp.exp(jnp.full((1, 1), heat_ref[0], jnp.float32))
    logits = own_pairs(low_ref[...].astype(jnp.float32), partner_low, heat, offset_ref[0])
    _, sigmoid = loss_and_sigmoid(-logits)
    grad_ref[...] = back_norm(unit, norm, sum_ref[...] + low(-sigmoid * heat) * partner_low)


def gradients(heat_exponent, offset_added, vectors, lows, partners, sums):
    return pl.pallas_call(
        grad_kernel,
        in_specs=[pl.BlockSpec(memory_space=pltpu.SMEM)] * 2 + [pl.BlockSpec(memory_space=pltpu.VMEM)] * 4,
        out_shape=jax.ShapeDtypeStruct(vectors.shape, jnp.float32),
    )(heat_exponent, offset_added, vectors, lows, partners, sums)


def swapped(value, axis, step):
    return lax.ppermute(value, axis, [(i, i ^ step) for i in range(lax.axis_size(axis))])


def doubled(value, axis, step):
    return jnp.concatenate([value, swapped(value, axis, step)], axis=0)


def halved(value, axis, step):
    half = value.shape[0] // 2
    sent = (value[half:] * HALF).astype(jnp.float16)
    return value[:half] + swapped(sent, axis, step).astype(jnp.float32) * (1 / HALF)


def summed(value, axis, steps):
    rows = value.shape[0] // (len(steps) + 1)
    blocks = [value[step * rows : (step + 1) * rows] for step in steps]
    arrived = [swapped((block * HALF).astype(jnp.float16), axis, step) for block, step in zip(blocks, steps)]
    return value[:rows] + sum(part.astype(jnp.float32) for part in arrived) * (1 / HALF)


def shards(picture_vectors, caption_vectors, heat_exponent, offset_added):
    rows, width = picture_vectors.shape
    plane, column = lax.axis_size(PLANE), lax.axis_size(COLUMN)
    steps = range(1, lax.axis_size("zl"))
    image_low, text_low, copies, own_loss = unit_rows(
        plane, heat_exponent, offset_added, picture_vectors, caption_vectors
    )

    other_low = jnp.broadcast_to(swapped(text_low, "zm", 1)[None], (plane, rows, width))
    texts = lax.all_to_all(lax.dynamic_update_slice(copies, other_low, (0, rows, 0)), PLANE, 0, 0)
    texts = texts.reshape(plane * 2 * rows, width)
    near = doubled(image_low, "zh", 1)
    near = jnp.concatenate([near] + [swapped(near, "zl", step) for step in steps], axis=0)
    far = swapped(near, "c", 1)

    place = (lax.axis_index(PLANE) * 2 * rows).astype(jnp.int32).reshape(1)
    weights, far_part, loss = pair_weights(place, heat_exponent, offset_added, own_loss, near, far, texts)
    far_part = swapped(far_part, "c", 1)
    near_part, text_part = pair_terms(weights, loss, near, far, texts)
    text_parts = lax.all_to_all(text_part.reshape(plane, 2 * rows, width + LANES), PLANE, 0, 0)
    image_sum = near_part + far_part
    image_sum = halved(summed(image_sum, "zl", steps), "zh", 1)

    plane_loss = jnp.sum(text_parts[:, 0, width : width + 3].astype(jnp.float32))
    losses = lax.all_to_all(jnp.broadcast_to(plane_loss, (column, 1, LANES)), COLUMN, 0, 0)
    text_sum = jnp.sum(text_parts[:, :, :width].astype(jnp.float32), axis=0)
    arrived = swapped((text_sum[rows:] * HALF).astype(jnp.float16), "zm", 1)
    arrived, losses = lax.optimization_barrier((arrived, losses))
    text_sum = text_sum[:rows] + arrived.astype(jnp.float32) * (1 / HALF)
    loss_mean = (jnp.sum(losses[:, 0, 0]) / (rows * lax.axis_size(AXES))).reshape(1)
    image_grads = gradients(heat_exponent, offset_added, picture_vectors, image_low, text_low, image_sum)
    text_grads = gradients(heat_exponent, offset_added, caption_vectors, text_low, image_low, text_sum)
    return (loss_mean, image_grads, text_grads)


def solution(mesh):
    fine = Mesh(mesh.devices.reshape(SIZES), AXES)
    in_specs = (P(AXES, None), P(AXES, None), P(), P())
    out_specs = (P(), P(AXES, None), P(AXES, None))
    return jax.shard_map(shards, mesh=fine, in_specs=in_specs, out_specs=out_specs, check_vma=False)
```

```python
import jax
import jax.numpy as jnp
from jax import lax
from jax.experimental import pallas as pl
from jax.experimental.pallas import tpu as pltpu
from jax.sharding import Mesh, PartitionSpec as P

epsilon = 1e-06
AXES = ("zm", "zl", "x", "c", "y", "zh")
SIZES = (2, 4, 4, 2, 4, 2)
PLANE = ("x", "y")
COLUMN = ("zm", "zl", "c", "zh")
LANES = 128
LIMIT = 20 * 1024 * 1024
HALF = 0.5


def normalize(raw_rows):
    row_norm = jnp.sqrt(jnp.sum(raw_rows * raw_rows, axis=1, keepdims=True) + epsilon)
    return (raw_rows / row_norm, row_norm)


def back_norm(unit_rows, row_norm, gradient):
    return (gradient - unit_rows * jnp.sum(unit_rows * gradient, axis=1, keepdims=True)) / row_norm


def low(rows):
    return rows.astype(jnp.bfloat16).astype(jnp.float32)


def loss_and_sigmoid(values):
    small = jnp.exp(-jnp.abs(values))
    loss = jnp.maximum(values, 0.0) + jnp.log1p(small)
    return loss, jnp.where(values >= 0, 1.0, small) / (1.0 + small)


def own_pairs(image_low, text_low, heat, offset):
    return jnp.sum(image_low * text_low, axis=1, keepdims=True) * heat + offset


def unit_kernel(heat_ref, offset_ref, picture_ref, caption_ref, image_ref, own_ref, text_ref, loss_ref):
    image_unit, _ = normalize(picture_ref[...])
    text_unit, _ = normalize(caption_ref[...])
    image_low, text_low = image_unit.astype(jnp.bfloat16), text_unit.astype(jnp.bfloat16)
    image_ref[...] = image_low
    text_ref[...] = jnp.broadcast_to(jnp.concatenate([text_low, text_low], axis=0)[None], text_ref.shape)
    own_ref[...] = text_low
    heat = jnp.exp(jnp.full((1, 1), heat_ref[0], jnp.float32))
    logits = own_pairs(image_low.astype(jnp.float32), text_low.astype(jnp.float32), heat, offset_ref[0])
    loss, _ = loss_and_sigmoid(-logits)
    loss_ref[...] = loss


def unit_rows(copies, heat_exponent, offset_added, pictures, captions):
    rows, width = pictures.shape
    return pl.pallas_call(
        unit_kernel,
        in_specs=[pl.BlockSpec(memory_space=pltpu.SMEM)] * 2 + [pl.BlockSpec(memory_space=pltpu.VMEM)] * 2,
        out_shape=[
            jax.ShapeDtypeStruct(pictures.shape, jnp.bfloat16),
            jax.ShapeDtypeStruct(captions.shape, jnp.bfloat16),
            jax.ShapeDtypeStruct((copies, 2 * rows, width), jnp.bfloat16),
            jax.ShapeDtypeStruct((rows, 1), jnp.float32),
        ],
    )(heat_exponent, offset_added, pictures, captions)


def pieces(total, shape):
    first = low(total)
    second = low(total - first)
    third = total - first - second
    lane = lax.broadcasted_iota(jnp.int32, shape, len(shape) - 1)
    spread = jnp.where(lane == 0, first, jnp.where(lane == 1, second, jnp.where(lane == 2, third, 0.0)))
    return spread.astype(jnp.bfloat16)


def pair_kernel(
    place_ref, heat_ref, offset_ref, own_loss_ref, near_ref, far_ref, text_ref, weight_ref, far_out_ref, loss_ref
):
    rows = own_loss_ref.shape[0]
    texts = text_ref[...]
    heat = jnp.exp(jnp.full((1, 1), heat_ref[0], jnp.float32))
    total = jnp.sum(own_loss_ref[...], axis=0, keepdims=True)
    for place, image_ref in enumerate((near_ref, far_ref)):
        logits = lax.dot_general(
            image_ref[...], texts, (((1,), (1,)), ((), ())), preferred_element_type=jnp.float32
        )
        logits = logits * heat + offset_ref[0]
        loss, sigmoid = loss_and_sigmoid(logits)
        weights = heat * sigmoid
        if image_ref is near_ref:
            image_row = lax.broadcasted_iota(jnp.int32, logits.shape, 0)
            text_row = lax.broadcasted_iota(jnp.int32, logits.shape, 1) - place_ref[0]
            match = (image_row == text_row) & (image_row < rows)
            weights = jnp.where(match, 0.0, weights)
            loss = jnp.where(match, 0.0, loss)
        weights = weights.astype(jnp.bfloat16)
        weight_ref[place] = weights
        total += jnp.sum(jnp.sum(loss, axis=0, keepdims=True), axis=1, keepdims=True)
    far_out_ref[...] = jnp.dot(weights, texts, preferred_element_type=jnp.float32)
    loss_ref[...] = jnp.broadcast_to(total, loss_ref.shape)


def pair_weights(place, heat_exponent, offset_added, own_loss, near, far, texts):
    half, width = near.shape
    count = texts.shape[0]
    return pl.pallas_call(
        pair_kernel,
        in_specs=[pl.BlockSpec(memory_space=pltpu.SMEM)] * 3 + [pl.BlockSpec(memory_space=pltpu.VMEM)] * 4,
        out_shape=[
            jax.ShapeDtypeStruct((2, half, count), jnp.bfloat16),
            jax.ShapeDtypeStruct((half, width), jnp.float32),
            jax.ShapeDtypeStruct((8, LANES), jnp.float32),
        ],
        compiler_params=pltpu.CompilerParams(vmem_limit_bytes=LIMIT),
        cost_estimate=pl.CostEstimate(
            flops=6 * half * count * width, bytes_accessed=8 * half * width, transcendentals=6 * half * count
        ),
    )(place, heat_exponent, offset_added, own_loss, near, far, texts)


def terms_kernel(weight_ref, loss_ref, near_ref, far_ref, text_ref, near_out_ref, text_out_ref):
    width = near_ref.shape[1]
    text_part = lax.dot_general(
        weight_ref[0], near_ref[...], (((0,), (0,)), ((), ())), preferred_element_type=jnp.float32
    )
    text_part += lax.dot_general(
        weight_ref[1], far_ref[...], (((0,), (0,)), ((), ())), preferred_element_type=jnp.float32
    )
    text_out_ref[:, :width] = text_part.astype(jnp.bfloat16)
    text_out_ref[:, width:] = pieces(loss_ref[:1, :1], (text_out_ref.shape[0], LANES))
    near_out_ref[...] = jnp.dot(weight_ref[0], text_ref[...], preferred_element_type=jnp.float32)


def pair_terms(weights, loss, near, far, texts):
    count, width = texts.shape
    return pl.pallas_call(
        terms_kernel,
        in_specs=[pl.BlockSpec(memory_space=pltpu.VMEM)] * 5,
        out_shape=[
            jax.ShapeDtypeStruct(near.shape, jnp.float32),
            jax.ShapeDtypeStruct((count, width + LANES), jnp.bfloat16),
        ],
        compiler_params=pltpu.CompilerParams(vmem_limit_bytes=LIMIT),
        cost_estimate=pl.CostEstimate(flops=3 * weights.size * width, bytes_accessed=16 * near.size, transcendentals=0),
    )(weights, loss, near, far, texts)


def grad_kernel(heat_ref, offset_ref, row_ref, low_ref, partner_ref, sum_ref, grad_ref):
    unit, norm = normalize(row_ref[...])
    partner_low = partner_ref[...].astype(jnp.float32)
    heat = jnp.exp(jnp.full((1, 1), heat_ref[0], jnp.float32))
    logits = own_pairs(low_ref[...].astype(jnp.float32), partner_low, heat, offset_ref[0])
    _, sigmoid = loss_and_sigmoid(-logits)
    grad_ref[...] = back_norm(unit, norm, sum_ref[...] + low(-sigmoid * heat) * partner_low)


def gradients(heat_exponent, offset_added, vectors, lows, partners, sums):
    return pl.pallas_call(
        grad_kernel,
        in_specs=[pl.BlockSpec(memory_space=pltpu.SMEM)] * 2 + [pl.BlockSpec(memory_space=pltpu.VMEM)] * 4,
        out_shape=jax.ShapeDtypeStruct(vectors.shape, jnp.float32),
    )(heat_exponent, offset_added, vectors, lows, partners, sums)


def swapped(value, axis, step):
    return lax.ppermute(value, axis, [(i, i ^ step) for i in range(lax.axis_size(axis))])


def doubled(value, axis, step):
    return jnp.concatenate([value, swapped(value, axis, step)], axis=0)


def halved(value, axis, step):
    half = value.shape[0] // 2
    sent = (value[half:] * HALF).astype(jnp.float16)
    return value[:half] + swapped(sent, axis, step).astype(jnp.float32) * (1 / HALF)


def shards(picture_vectors, caption_vectors, heat_exponent, offset_added):
    rows, width = picture_vectors.shape
    plane, column = lax.axis_size(PLANE), lax.axis_size(COLUMN)
    steps = [1 << bit for bit in range(lax.axis_size("zl").bit_length() - 1)]
    image_low, text_low, copies, own_loss = unit_rows(
        plane, heat_exponent, offset_added, picture_vectors, caption_vectors
    )

    other_low = jnp.broadcast_to(swapped(text_low, "zm", 1)[None], (plane, rows, width))
    texts = lax.all_to_all(lax.dynamic_update_slice(copies, other_low, (0, rows, 0)), PLANE, 0, 0)
    texts = texts.reshape(plane * 2 * rows, width)
    near = doubled(image_low, "zh", 1)
    for step in reversed(steps):
        near = doubled(near, "zl", step)
    far = swapped(near, "c", 1)

    place = (lax.axis_index(PLANE) * 2 * rows).astype(jnp.int32).reshape(1)
    weights, far_part, loss = pair_weights(place, heat_exponent, offset_added, own_loss, near, far, texts)
    far_part = swapped(far_part, "c", 1)
    near_part, text_part = pair_terms(weights, loss, near, far, texts)
    text_parts = lax.all_to_all(text_part.reshape(plane, 2 * rows, width + LANES), PLANE, 0, 0)
    image_sum = near_part + far_part
    for step in steps:
        image_sum = halved(image_sum, "zl", step)
    image_sum = halved(image_sum, "zh", 1)

    plane_loss = jnp.sum(text_parts[:, 0, width : width + 3].astype(jnp.float32))
    losses = lax.all_to_all(jnp.broadcast_to(plane_loss, (column, 1, LANES)), COLUMN, 0, 0)
    text_sum = jnp.sum(text_parts[:, :, :width].astype(jnp.float32), axis=0)
    arrived = swapped((text_sum[rows:] * HALF).astype(jnp.float16), "zm", 1)
    arrived, losses = lax.optimization_barrier((arrived, losses))
    text_sum = text_sum[:rows] + arrived.astype(jnp.float32) * (1 / HALF)
    loss_mean = (jnp.sum(losses[:, 0, 0]) / (rows * lax.axis_size(AXES))).reshape(1)
    image_grads = gradients(heat_exponent, offset_added, picture_vectors, image_low, text_low, image_sum)
    text_grads = gradients(heat_exponent, offset_added, caption_vectors, text_low, image_low, text_sum)
    return (loss_mean, image_grads, text_grads)


def solution(mesh):
    fine = Mesh(mesh.devices.reshape(SIZES), AXES)
    in_specs = (P(AXES, None), P(AXES, None), P(), P())
    out_specs = (P(), P(AXES, None), P(AXES, None))
    return jax.shard_map(shards, mesh=fine, in_specs=in_specs, out_specs=out_specs, check_vma=False)
```

```python
import jax
import jax.numpy as jnp
from jax import lax
from jax.experimental import pallas as pl
from jax.experimental.pallas import tpu as pltpu
from jax.sharding import Mesh, PartitionSpec as P

epsilon = 1e-06
AXES = ("zm", "zl", "x", "c", "y", "zh")
SIZES = (2, 4, 4, 2, 4, 2)
PLANE = ("x", "y")
COLUMN = ("zm", "zl", "c", "zh")
LANES = 128
LIMIT = 20 * 1024 * 1024
HALF = 0.5


def normalize(raw_rows):
    row_norm = jnp.sqrt(jnp.sum(raw_rows * raw_rows, axis=1, keepdims=True) + epsilon)
    return (raw_rows / row_norm, row_norm)


def back_norm(unit_rows, row_norm, gradient):
    return (gradient - unit_rows * jnp.sum(unit_rows * gradient, axis=1, keepdims=True)) / row_norm


def low(rows):
    return rows.astype(jnp.bfloat16).astype(jnp.float32)


def loss_and_sigmoid(values):
    small = jnp.exp(-jnp.abs(values))
    loss = jnp.maximum(values, 0.0) + jnp.log1p(small)
    return loss, jnp.where(values >= 0, 1.0, small) / (1.0 + small)


def own_pairs(image_low, text_low, heat, offset):
    return jnp.sum(image_low * text_low, axis=1, keepdims=True) * heat + offset


def unit_kernel(heat_ref, offset_ref, picture_ref, caption_ref, image_ref, own_ref, text_ref, loss_ref):
    image_unit, _ = normalize(picture_ref[...])
    text_unit, _ = normalize(caption_ref[...])
    image_low, text_low = image_unit.astype(jnp.bfloat16), text_unit.astype(jnp.bfloat16)
    image_ref[...] = image_low
    text_ref[...] = jnp.broadcast_to(jnp.concatenate([text_low, text_low], axis=0)[None], text_ref.shape)
    own_ref[...] = text_low
    heat = jnp.exp(jnp.full((1, 1), heat_ref[0], jnp.float32))
    logits = own_pairs(image_low.astype(jnp.float32), text_low.astype(jnp.float32), heat, offset_ref[0])
    loss, _ = loss_and_sigmoid(-logits)
    loss_ref[...] = loss


def unit_rows(copies, heat_exponent, offset_added, pictures, captions):
    rows, width = pictures.shape
    return pl.pallas_call(
        unit_kernel,
        in_specs=[pl.BlockSpec(memory_space=pltpu.SMEM)] * 2 + [pl.BlockSpec(memory_space=pltpu.VMEM)] * 2,
        out_shape=[
            jax.ShapeDtypeStruct(pictures.shape, jnp.bfloat16),
            jax.ShapeDtypeStruct(captions.shape, jnp.bfloat16),
            jax.ShapeDtypeStruct((copies, 2 * rows, width), jnp.bfloat16),
            jax.ShapeDtypeStruct((rows, 1), jnp.float32),
        ],
    )(heat_exponent, offset_added, pictures, captions)


def pieces(total, shape):
    first = low(total)
    second = low(total - first)
    third = total - first - second
    lane = lax.broadcasted_iota(jnp.int32, shape, len(shape) - 1)
    spread = jnp.where(lane == 0, first, jnp.where(lane == 1, second, jnp.where(lane == 2, third, 0.0)))
    return spread.astype(jnp.bfloat16)


def pair_kernel(
    place_ref, heat_ref, offset_ref, own_loss_ref, near_ref, far_ref, text_ref, weight_ref, far_out_ref, loss_ref
):
    rows = own_loss_ref.shape[0]
    texts = text_ref[...]
    heat = jnp.exp(jnp.full((1, 1), heat_ref[0], jnp.float32))
    total = jnp.sum(own_loss_ref[...], axis=0, keepdims=True)
    for place, image_ref in enumerate((near_ref, far_ref)):
        logits = lax.dot_general(
            image_ref[...], texts, (((1,), (1,)), ((), ())), preferred_element_type=jnp.float32
        )
        logits = logits * heat + offset_ref[0]
        loss, sigmoid = loss_and_sigmoid(logits)
        weights = heat * sigmoid
        if image_ref is near_ref:
            image_row = lax.broadcasted_iota(jnp.int32, logits.shape, 0)
            text_row = lax.broadcasted_iota(jnp.int32, logits.shape, 1) - place_ref[0]
            match = (image_row == text_row) & (image_row < rows)
            weights = jnp.where(match, 0.0, weights)
            loss = jnp.where(match, 0.0, loss)
        weights = weights.astype(jnp.bfloat16)
        weight_ref[place] = weights
        total += jnp.sum(jnp.sum(loss, axis=0, keepdims=True), axis=1, keepdims=True)
    far_out_ref[...] = jnp.dot(weights, texts, preferred_element_type=jnp.float32)
    loss_ref[...] = jnp.broadcast_to(total, loss_ref.shape)


def pair_weights(place, heat_exponent, offset_added, own_loss, near, far, texts):
    half, width = near.shape
    count = texts.shape[0]
    return pl.pallas_call(
        pair_kernel,
        in_specs=[pl.BlockSpec(memory_space=pltpu.SMEM)] * 3 + [pl.BlockSpec(memory_space=pltpu.VMEM)] * 4,
        out_shape=[
            jax.ShapeDtypeStruct((2, half, count), jnp.bfloat16),
            jax.ShapeDtypeStruct((half, width), jnp.float32),
            jax.ShapeDtypeStruct((8, LANES), jnp.float32),
        ],
        compiler_params=pltpu.CompilerParams(vmem_limit_bytes=LIMIT),
        cost_estimate=pl.CostEstimate(
            flops=6 * half * count * width, bytes_accessed=8 * half * width, transcendentals=6 * half * count
        ),
    )(place, heat_exponent, offset_added, own_loss, near, far, texts)


def terms_kernel(weight_ref, loss_ref, near_ref, far_ref, text_ref, near_out_ref, text_out_ref):
    width = near_ref.shape[1]
    text_part = lax.dot_general(
        weight_ref[0], near_ref[...], (((0,), (0,)), ((), ())), preferred_element_type=jnp.float32
    )
    text_part += lax.dot_general(
        weight_ref[1], far_ref[...], (((0,), (0,)), ((), ())), preferred_element_type=jnp.float32
    )
    text_out_ref[:, :width] = text_part.astype(jnp.bfloat16)
    text_out_ref[:, width:] = pieces(loss_ref[:1, :1], (text_out_ref.shape[0], LANES))
    near_out_ref[...] = jnp.dot(weight_ref[0], text_ref[...], preferred_element_type=jnp.float32)


def pair_terms(weights, loss, near, far, texts):
    count, width = texts.shape
    return pl.pallas_call(
        terms_kernel,
        in_specs=[pl.BlockSpec(memory_space=pltpu.VMEM)] * 5,
        out_shape=[
            jax.ShapeDtypeStruct(near.shape, jnp.float32),
            jax.ShapeDtypeStruct((count, width + LANES), jnp.bfloat16),
        ],
        compiler_params=pltpu.CompilerParams(vmem_limit_bytes=LIMIT),
        cost_estimate=pl.CostEstimate(flops=3 * weights.size * width, bytes_accessed=16 * near.size, transcendentals=0),
    )(weights, loss, near, far, texts)


def grad_kernel(heat_ref, offset_ref, row_ref, low_ref, partner_ref, sum_ref, grad_ref):
    unit, norm = normalize(row_ref[...])
    partner_low = partner_ref[...].astype(jnp.float32)
    heat = jnp.exp(jnp.full((1, 1), heat_ref[0], jnp.float32))
    logits = own_pairs(low_ref[...].astype(jnp.float32), partner_low, heat, offset_ref[0])
    _, sigmoid = loss_and_sigmoid(-logits)
    grad_ref[...] = back_norm(unit, norm, sum_ref[...] + low(-sigmoid * heat) * partner_low)


def gradients(heat_exponent, offset_added, vectors, lows, partners, sums):
    return pl.pallas_call(
        grad_kernel,
        in_specs=[pl.BlockSpec(memory_space=pltpu.SMEM)] * 2 + [pl.BlockSpec(memory_space=pltpu.VMEM)] * 4,
        out_shape=jax.ShapeDtypeStruct(vectors.shape, jnp.float32),
    )(heat_exponent, offset_added, vectors, lows, partners, sums)


def swapped(value, axis, step):
    return lax.ppermute(value, axis, [(i, i ^ step) for i in range(lax.axis_size(axis))])


def doubled(value, axis, step):
    return jnp.concatenate([value, swapped(value, axis, step)], axis=0)


def halved(value, axis, step):
    half = value.shape[0] // 2
    sent = (value[half:] * HALF).astype(jnp.float16)
    return value[:half] + swapped(sent, axis, step).astype(jnp.float32) * (1 / HALF)


def shards(picture_vectors, caption_vectors, heat_exponent, offset_added):
    rows, width = picture_vectors.shape
    plane, column = lax.axis_size(PLANE), lax.axis_size(COLUMN)
    steps = [1 << bit for bit in range(lax.axis_size("zl").bit_length() - 1)]
    image_low, text_low, copies, own_loss = unit_rows(
        plane, heat_exponent, offset_added, picture_vectors, caption_vectors
    )

    other_low = swapped(text_low, "zm", 1)
    other_low, near = lax.optimization_barrier((other_low, image_low))
    other_low = jnp.broadcast_to(other_low[None], (plane, rows, width))
    texts = lax.all_to_all(lax.dynamic_update_slice(copies, other_low, (0, rows, 0)), PLANE, 0, 0)
    texts = texts.reshape(plane * 2 * rows, width)
    near = doubled(near, "zh", 1)
    near = jnp.concatenate([near] + [swapped(near, "zl", step) for step in (2, 1, 3)], axis=0)
    far = swapped(near, "c", 1)

    place = (lax.axis_index(PLANE) * 2 * rows).astype(jnp.int32).reshape(1)
    weights, far_part, loss = pair_weights(place, heat_exponent, offset_added, own_loss, near, far, texts)
    far_part = swapped(far_part, "c", 1)
    near_part, text_part = pair_terms(weights, loss, near, far, texts)
    text_parts = lax.all_to_all(text_part.reshape(plane, 2 * rows, width + LANES), PLANE, 0, 0)
    image_sum = near_part + far_part
    for step in steps:
        image_sum = halved(image_sum, "zl", step)
    image_sum = halved(image_sum, "zh", 1)

    plane_loss = jnp.sum(text_parts[:, 0, width : width + 3].astype(jnp.float32))
    losses = lax.all_to_all(jnp.broadcast_to(plane_loss, (column, 1, LANES)), COLUMN, 0, 0)
    text_sum = jnp.sum(text_parts[:, :, :width].astype(jnp.float32), axis=0)
    arrived = swapped((text_sum[rows:] * HALF).astype(jnp.float16), "zm", 1)
    arrived, losses = lax.optimization_barrier((arrived, losses))
    text_sum = text_sum[:rows] + arrived.astype(jnp.float32) * (1 / HALF)
    loss_mean = (jnp.sum(losses[:, 0, 0]) / (rows * lax.axis_size(AXES))).reshape(1)
    image_grads = gradients(heat_exponent, offset_added, picture_vectors, image_low, text_low, image_sum)
    text_grads = gradients(heat_exponent, offset_added, caption_vectors, text_low, image_low, text_sum)
    return (loss_mean, image_grads, text_grads)


def solution(mesh):
    fine = Mesh(mesh.devices.reshape(SIZES), AXES)
    in_specs = (P(AXES, None), P(AXES, None), P(), P())
    out_specs = (P(), P(AXES, None), P(AXES, None))
    return jax.shard_map(shards, mesh=fine, in_specs=in_specs, out_specs=out_specs, check_vma=False)
```

```python
import jax
import jax.numpy as jnp
from jax import lax
from jax.experimental import pallas as pl
from jax.experimental.pallas import tpu as pltpu
from jax.sharding import Mesh, PartitionSpec as P

epsilon = 1e-06
AXES = ("zm", "zl", "x", "c", "y", "zh")
SIZES = (2, 4, 4, 2, 4, 2)
PLANE = ("x", "y")
COLUMN = ("zm", "zl", "c", "zh")
LANES = 128
LIMIT = 20 * 1024 * 1024
HALF = 0.5


def normalize(raw_rows):
    row_norm = jnp.sqrt(jnp.sum(raw_rows * raw_rows, axis=1, keepdims=True) + epsilon)
    return (raw_rows / row_norm, row_norm)


def back_norm(unit_rows, row_norm, gradient):
    return (gradient - unit_rows * jnp.sum(unit_rows * gradient, axis=1, keepdims=True)) / row_norm


def low(rows):
    return rows.astype(jnp.bfloat16).astype(jnp.float32)


def loss_and_sigmoid(values):
    small = jnp.exp(-jnp.abs(values))
    loss = jnp.maximum(values, 0.0) + jnp.log1p(small)
    return loss, jnp.where(values >= 0, 1.0, small) / (1.0 + small)


def own_pairs(image_low, text_low, heat, offset):
    return jnp.sum(image_low * text_low, axis=1, keepdims=True) * heat + offset


def unit_kernel(heat_ref, offset_ref, picture_ref, caption_ref, image_ref, own_ref, text_ref, loss_ref):
    image_unit, _ = normalize(picture_ref[...])
    text_unit, _ = normalize(caption_ref[...])
    image_low, text_low = image_unit.astype(jnp.bfloat16), text_unit.astype(jnp.bfloat16)
    image_ref[...] = image_low
    text_ref[...] = jnp.broadcast_to(jnp.concatenate([text_low, text_low], axis=0)[None], text_ref.shape)
    own_ref[...] = text_low
    heat = jnp.exp(jnp.full((1, 1), heat_ref[0], jnp.float32))
    logits = own_pairs(image_low.astype(jnp.float32), text_low.astype(jnp.float32), heat, offset_ref[0])
    loss, _ = loss_and_sigmoid(-logits)
    loss_ref[...] = loss


def unit_rows(copies, heat_exponent, offset_added, pictures, captions):
    rows, width = pictures.shape
    return pl.pallas_call(
        unit_kernel,
        in_specs=[pl.BlockSpec(memory_space=pltpu.SMEM)] * 2 + [pl.BlockSpec(memory_space=pltpu.VMEM)] * 2,
        out_shape=[
            jax.ShapeDtypeStruct(pictures.shape, jnp.bfloat16),
            jax.ShapeDtypeStruct(captions.shape, jnp.bfloat16),
            jax.ShapeDtypeStruct((copies, 2 * rows, width), jnp.bfloat16),
            jax.ShapeDtypeStruct((rows, 1), jnp.float32),
        ],
    )(heat_exponent, offset_added, pictures, captions)


def pieces(total, shape):
    first = low(total)
    second = low(total - first)
    third = total - first - second
    lane = lax.broadcasted_iota(jnp.int32, shape, len(shape) - 1)
    spread = jnp.where(lane == 0, first, jnp.where(lane == 1, second, jnp.where(lane == 2, third, 0.0)))
    return spread.astype(jnp.bfloat16)


def pair_kernel(
    place_ref, heat_ref, offset_ref, own_loss_ref, near_ref, far_ref, text_ref, weight_ref, far_out_ref, loss_ref
):
    rows = own_loss_ref.shape[0]
    texts = text_ref[...]
    heat = jnp.exp(jnp.full((1, 1), heat_ref[0], jnp.float32))
    total = jnp.sum(own_loss_ref[...], axis=0, keepdims=True)
    for place, image_ref in enumerate((near_ref, far_ref)):
        logits = lax.dot_general(
            image_ref[...], texts, (((1,), (1,)), ((), ())), preferred_element_type=jnp.float32
        )
        logits = logits * heat + offset_ref[0]
        loss, sigmoid = loss_and_sigmoid(logits)
        weights = heat * sigmoid
        if image_ref is near_ref:
            image_row = lax.broadcasted_iota(jnp.int32, logits.shape, 0)
            text_row = lax.broadcasted_iota(jnp.int32, logits.shape, 1) - place_ref[0]
            match = (image_row == text_row) & (image_row < rows)
            weights = jnp.where(match, 0.0, weights)
            loss = jnp.where(match, 0.0, loss)
        weights = weights.astype(jnp.bfloat16)
        weight_ref[place] = weights
        total += jnp.sum(jnp.sum(loss, axis=0, keepdims=True), axis=1, keepdims=True)
    far_out_ref[...] = jnp.dot(weights, texts, preferred_element_type=jnp.float32)
    loss_ref[...] = jnp.broadcast_to(total, loss_ref.shape)


def pair_weights(place, heat_exponent, offset_added, own_loss, near, far, texts):
    half, width = near.shape
    count = texts.shape[0]
    return pl.pallas_call(
        pair_kernel,
        in_specs=[pl.BlockSpec(memory_space=pltpu.SMEM)] * 3 + [pl.BlockSpec(memory_space=pltpu.VMEM)] * 4,
        out_shape=[
            jax.ShapeDtypeStruct((2, half, count), jnp.bfloat16),
            jax.ShapeDtypeStruct((half, width), jnp.float32),
            jax.ShapeDtypeStruct((8, LANES), jnp.float32),
        ],
        compiler_params=pltpu.CompilerParams(vmem_limit_bytes=LIMIT),
        cost_estimate=pl.CostEstimate(
            flops=6 * half * count * width, bytes_accessed=8 * half * width, transcendentals=6 * half * count
        ),
    )(place, heat_exponent, offset_added, own_loss, near, far, texts)


def terms_kernel(weight_ref, loss_ref, near_ref, far_ref, text_ref, near_out_ref, text_out_ref):
    width = near_ref.shape[1]
    text_part = lax.dot_general(
        weight_ref[0], near_ref[...], (((0,), (0,)), ((), ())), preferred_element_type=jnp.float32
    )
    text_part += lax.dot_general(
        weight_ref[1], far_ref[...], (((0,), (0,)), ((), ())), preferred_element_type=jnp.float32
    )
    text_out_ref[:, :width] = text_part.astype(jnp.bfloat16)
    text_out_ref[:, width:] = pieces(loss_ref[:1, :1], (text_out_ref.shape[0], LANES))
    near_out_ref[...] = jnp.dot(weight_ref[0], text_ref[...], preferred_element_type=jnp.float32)


def pair_terms(weights, loss, near, far, texts):
    count, width = texts.shape
    return pl.pallas_call(
        terms_kernel,
        in_specs=[pl.BlockSpec(memory_space=pltpu.VMEM)] * 5,
        out_shape=[
            jax.ShapeDtypeStruct(near.shape, jnp.float32),
            jax.ShapeDtypeStruct((count, width + LANES), jnp.bfloat16),
        ],
        compiler_params=pltpu.CompilerParams(vmem_limit_bytes=LIMIT),
        cost_estimate=pl.CostEstimate(flops=3 * weights.size * width, bytes_accessed=16 * near.size, transcendentals=0),
    )(weights, loss, near, far, texts)


def grad_kernel(heat_ref, offset_ref, row_ref, low_ref, partner_ref, sum_ref, grad_ref):
    unit, norm = normalize(row_ref[...])
    partner_low = partner_ref[...].astype(jnp.float32)
    heat = jnp.exp(jnp.full((1, 1), heat_ref[0], jnp.float32))
    logits = own_pairs(low_ref[...].astype(jnp.float32), partner_low, heat, offset_ref[0])
    _, sigmoid = loss_and_sigmoid(-logits)
    grad_ref[...] = back_norm(unit, norm, sum_ref[...] + low(-sigmoid * heat) * partner_low)


def gradients(heat_exponent, offset_added, vectors, lows, partners, sums):
    return pl.pallas_call(
        grad_kernel,
        in_specs=[pl.BlockSpec(memory_space=pltpu.SMEM)] * 2 + [pl.BlockSpec(memory_space=pltpu.VMEM)] * 4,
        out_shape=jax.ShapeDtypeStruct(vectors.shape, jnp.float32),
    )(heat_exponent, offset_added, vectors, lows, partners, sums)


def loss_kernel(part_ref, loss_ref):
    width = part_ref.shape[2] - LANES
    terms = jnp.sum(part_ref[:, :16, width:].astype(jnp.float32), axis=0)[:8]
    lane = lax.broadcasted_iota(jnp.int32, terms.shape, 1)
    total = jnp.sum(jnp.where(lane < 3, terms, 0.0), axis=1, keepdims=True)
    loss_ref[...] = jnp.broadcast_to(total[None], loss_ref.shape)


def loss_copies(count, parts):
    return pl.pallas_call(
        loss_kernel,
        in_specs=[pl.BlockSpec(memory_space=pltpu.VMEM)],
        out_shape=jax.ShapeDtypeStruct((count, 8, LANES), jnp.float32),
        compiler_params=pltpu.CompilerParams(vmem_limit_bytes=LIMIT),
    )(parts)


def swapped(value, axis, step):
    return lax.ppermute(value, axis, [(i, i ^ step) for i in range(lax.axis_size(axis))])


def doubled(value, axis, step):
    return jnp.concatenate([value, swapped(value, axis, step)], axis=0)


def halved(value, axis, step):
    half = value.shape[0] // 2
    sent = (value[half:] * HALF).astype(jnp.float16)
    return value[:half] + swapped(sent, axis, step).astype(jnp.float32) * (1 / HALF)


def shards(picture_vectors, caption_vectors, heat_exponent, offset_added):
    rows, width = picture_vectors.shape
    plane, column = lax.axis_size(PLANE), lax.axis_size(COLUMN)
    steps = [1 << bit for bit in range(lax.axis_size("zl").bit_length() - 1)]
    image_low, text_low, copies, own_loss = unit_rows(
        plane, heat_exponent, offset_added, picture_vectors, caption_vectors
    )

    other_low = jnp.broadcast_to(swapped(text_low, "zm", 1)[None], (plane, rows, width))
    texts = lax.all_to_all(lax.dynamic_update_slice(copies, other_low, (0, rows, 0)), PLANE, 0, 0)
    texts = texts.reshape(plane * 2 * rows, width)
    near = doubled(image_low, "zh", 1)
    for step in reversed(steps):
        near = doubled(near, "zl", step)
    far = swapped(near, "c", 1)

    place = (lax.axis_index(PLANE) * 2 * rows).astype(jnp.int32).reshape(1)
    weights, far_part, loss = pair_weights(place, heat_exponent, offset_added, own_loss, near, far, texts)
    far_part = swapped(far_part, "c", 1)
    near_part, text_part = pair_terms(weights, loss, near, far, texts)
    text_parts = lax.all_to_all(text_part.reshape(plane, 2 * rows, width + LANES), PLANE, 0, 0)
    image_sum = near_part + far_part
    for step in steps:
        image_sum = halved(image_sum, "zl", step)
    image_sum = halved(image_sum, "zh", 1)

    losses = lax.all_to_all(loss_copies(column, text_parts), COLUMN, 0, 0)
    text_sum = jnp.sum(text_parts[:, :, :width].astype(jnp.float32), axis=0)
    arrived = swapped((text_sum[rows:] * HALF).astype(jnp.float16), "zm", 1)
    arrived, losses = lax.optimization_barrier((arrived, losses))
    text_sum = text_sum[:rows] + arrived.astype(jnp.float32) * (1 / HALF)
    loss_mean = (jnp.sum(losses[:, 0, 0]) / (rows * lax.axis_size(AXES))).reshape(1)
    image_grads = gradients(heat_exponent, offset_added, picture_vectors, image_low, text_low, image_sum)
    text_grads = gradients(heat_exponent, offset_added, caption_vectors, text_low, image_low, text_sum)
    return (loss_mean, image_grads, text_grads)


def solution(mesh):
    fine = Mesh(mesh.devices.reshape(SIZES), AXES)
    in_specs = (P(AXES, None), P(AXES, None), P(), P())
    out_specs = (P(), P(AXES, None), P(AXES, None))
    return jax.shard_map(shards, mesh=fine, in_specs=in_specs, out_specs=out_specs, check_vma=False)
```
